32 devices in a mesh: parts: 2 (over x), sta: 16 (over z, y, core).
Axes of the slice: x: 2, y: 2, z: 4, core: 2. Of those that a mesh axis runs over, the one named last changes fastest.
Arguments:
- data: bfloat16 [32, 3, 896], P(('parts', 'sta')), parts along dimension 0, may hold values from -40 to 40
- templates: bfloat16 [128, 3, 512], P('sta'), may hold values from -12 to 12
- station_lists: int32 [16, 128], replicated, may hold values from 0 to 15, as said below
- counts: int32 [128], replicated, may hold values from 8 to 16
- offsets: int32 [16, 128], replicated, may hold values from 0 to 127
Outputs:
- detection: float32 [256, 256], P(('parts', 'sta')), parts along dimension 0
The draws below stay inside these ranges and needn't reach their ends.
There are 2 independent parts, one for each index of `parts`. The reference program is written for one: setup_inputs(seed, part) draws one part's arguments, and reference() takes and returns one part's arrays. A program takes and returns all parts, laid end to end along the dimension named above; an argument that names none is the same for every part. Nothing has to cross between parts.
Inputs may be any that keep to these rules, and one draw needn't show every extreme that they name: `station_lists`: each column names every one of the 16 stations once; template t uses the stations in entries k < counts[t] of its column. offsets[k, t] belongs to the station in entry k of template t's column.
All inputs are finite; a program needn't handle non-finite values.
Results may differ from the reference program's by a relative error of at most 0.0028.
Values may be sent and summed in bfloat16 or wider, within the bound.
A program may use at most 64 MiB of HBM per device.

```python
import math
import jax
import jax.numpy as jnp
from jax import lax

NCH = 3
L = 512
OFFMAX = 128
NTAU = 256
NSTA = 16
NT = 128
NS = 896


def draw_data(key, part):
    key_list = jax.random.split(key, 2)
    noise_part = jnp.clip(jax.random.normal(key_list[0], (NSTA, NCH, NS), jnp.float32), -4.0, 4.0)
    levels = jax.random.uniform(key_list[1], (NSTA, NCH, NS // 64, 1), jnp.float32, 0.0, math.log(10.0))
    envelope = jnp.broadcast_to(jnp.exp(levels), (NSTA, NCH, NS // 64, 64)).reshape(NSTA, NCH, NS)
    return (noise_part * envelope).astype(jnp.bfloat16)


def draw_templates(key, part):
    key_list = jax.random.split(key, 2)
    levels = jax.random.uniform(key_list[1], (NT, NCH, 1), jnp.float32, math.log(0.3), math.log(3.0))
    wave_part = jnp.clip(jax.random.normal(key_list[0], (NT, NCH, L), jnp.float32), -4.0, 4.0)
    return (wave_part * jnp.exp(levels)).astype(jnp.bfloat16)


def draw_station_lists(key, part):
    key_list = jax.random.split(jax.random.fold_in(key, 17), NT)
    columns = jax.vmap(lambda sub_key: jax.random.permutation(sub_key, NSTA))(key_list)
    return columns.T.astype(jnp.int32)


def draw_counts(key, part):
    key_list = jax.random.split(key, 3)
    values = jax.random.randint(key_list[0], (NT,), NSTA // 2, NSTA + 1, dtype=jnp.int32)
    top_slot = jax.random.randint(key_list[1], (), 0, NT, dtype=jnp.int32)
    low_slot = (top_slot + 1 + jax.random.randint(key_list[2], (), 0, NT - 1, dtype=jnp.int32)) % NT
    return values.at[top_slot].set(NSTA).at[low_slot].set(NSTA // 2)


def place_ends(values, key, low, top_value):
    place = [jax.random.randint(jax.random.fold_in(key, axis), (), 0, length) for axis, length in enumerate(values.shape)]
    longest = values.shape.index(max(values.shape))
    next_to = place[:longest] + [(place[longest] + 1) % values.shape[longest]] + place[longest + 1:]
    return values.at[tuple(place)].set(low).at[tuple(next_to)].set(top_value)


def setup_inputs(seed: int = 0, part: int = 0) -> dict:
    streams_of = jax.random.split(jax.random.key(seed), 6)
    part_splits = jax.random.split(jax.random.fold_in(streams_of[5], part), 6)
    return {
        "data": draw_data(jax.random.fold_in(jax.random.fold_in(streams_of[5], part), 71), part),
        "templates": draw_templates(jax.random.fold_in(streams_of[5], 71), part),
        "station_lists": draw_station_lists(jax.random.fold_in(streams_of[5], 71), part),
        "counts": draw_counts(jax.random.fold_in(streams_of[5], 71), part),
        "offsets": place_ends(jax.random.randint(streams_of[4], (NSTA, NT), 0, OFFMAX), jax.random.fold_in(streams_of[4], 1), 0, OFFMAX - 1).astype(jnp.int32),
    }


def reference(data, templates, station_lists, counts, offsets):
    lag_count = NTAU + OFFMAX
    lists_rows = station_lists.T
    offset_rows = offsets.T
    values = templates.astype(jnp.float32)
    centered = (values - lax.optimization_barrier(jnp.mean(values, axis=2, keepdims=True))).astype(jnp.bfloat16)
    cen_values = centered.astype(jnp.float32)
    chan_norms = jnp.sqrt(lax.optimization_barrier(jnp.mean(cen_values * cen_values, axis=2)) + 1e-06)
    samples = data.astype(jnp.float32)
    window_sum = lax.reduce_window(samples, 0.0, lax.add, (1, 1, L), (1, 1, 1), 'VALID')[:, :, :lag_count]
    square_sum = lax.reduce_window(samples * samples, 0.0, lax.add, (1, 1, L), (1, 1, 1), 'VALID')[:, :, :lag_count]
    mean_one = window_sum / L
    mean_two = square_sum / L
    scales = jnp.sqrt(mean_two - mean_one * mean_one + 1e-05)
    row_index = jnp.arange(NT, dtype=jnp.int32)[:, None]
    in_count = jnp.arange(NSTA, dtype=jnp.int32)[None, :] < counts[:, None]
    member = jnp.zeros((NT, NSTA), jnp.float32).at[row_index, lists_rows].set(in_count.astype(jnp.float32))
    shift_table = jnp.zeros((NT, NSTA), jnp.int32).at[row_index, lists_rows].set(jnp.where(in_count, offset_rows, 0).astype(jnp.int32))
    hankel_index = jnp.arange(lag_count, dtype=jnp.int32)[:, None] + jnp.arange(L, dtype=jnp.int32)[None, :]
    lag_index = jnp.arange(NTAU, dtype=jnp.int32)[None, :]

    def station_step(running, inputs):
        station_samples, station_scales, station_member, station_shift = inputs
        hankel = station_samples[:, hankel_index].astype(jnp.float32)
        products = jnp.einsum('tck,cuk->tcu', cen_values, hankel)
        normalized = products / (L * chan_norms[:, :, None] * station_scales[None])
        fitted = lax.optimization_barrier(jnp.mean(normalized, axis=1))
        picked = jnp.take_along_axis(fitted, lag_index + station_shift[:, None], axis=1)
        return (running + station_member[:, None] * picked, None)
    zero_rows = jnp.zeros((NT, NTAU), jnp.float32)
    stacked, _ = lax.scan(station_step, zero_rows, (data, scales, member.T, shift_table.T))
    return stacked
```

```python
import functools

import jax
import jax.numpy as jnp
from jax import lax
from jax.experimental import pallas as pl
from jax.experimental.pallas import tpu as pltpu
from jax.sharding import PartitionSpec as P

NCH = 3
L = 512
NTAU = 256
LANES = 128
ROWS = 8
LAGS = 32
SUB = LANES // LAGS
F32 = jnp.float32
BF16 = jnp.bfloat16
MESH = pl.DeviceIdType.MESH


def network_kernel(
    n, data_hbm, templates_hbm, lists_hbm, counts_hbm, offsets_hbm, out_ref,
    templates_ref, lists_ref, counts_ref, offsets_ref,
    slots, staged, bands, factors_ref, window_ref, lane_codes, sources,
    fetch_sem, send_sem, recv_sem, late_sem,
):
    me = lax.axis_index("sta")
    fetches = [
        pltpu.make_async_copy(source, target, fetch_sem.at[i])
        for i, (source, target) in enumerate(
            [
                (data_hbm.at[0], slots.at[me]), (templates_hbm, templates_ref), (lists_hbm, lists_ref),
                (counts_hbm, counts_ref), (offsets_hbm, offsets_ref),
            ]
        )
    ]
    fetches[0].start()
    samples_len = data_hbm.shape[2]
    blocks = samples_len // LANES
    lag_blocks = (samples_len - L) // LANES
    wave_blocks = L // LANES
    depth = L + LANES
    own = templates_ref.shape[1]
    groups = own // SUB
    station_rows = ROWS * blocks
    parts_of_lags = lag_blocks * SUB

    late_from = n - n // 4
    early = me < late_from
    barrier = pltpu.get_barrier_semaphore()

    def to_others(low, high, act):
        for d in range(low, high):
            pl.when(me != d)(functools.partial(act, d))

    def greet(d):
        pl.semaphore_signal(barrier, inc=1, device_id={"sta": jnp.int32(d)}, device_id_type=MESH)

    def announce(d):
        pl.semaphore_signal(late_sem, inc=1, device_id={"sta": jnp.int32(d)}, device_id_type=MESH)

    to_others(late_from, n, greet)

    @pl.when(early)
    def _():
        to_others(0, late_from, greet)

    for fetch in fetches[1:]:
        fetch.start()

    def copy_to(target):
        return pltpu.make_async_remote_copy(
            src_ref=slots.at[me],
            dst_ref=slots.at[me],
            send_sem=send_sem.at[target],
            recv_sem=recv_sem.at[me],
            device_id={"sta": target},
            device_id_type=MESH,
        )

    def send(d):
        copy_to(jnp.int32(d)).start()

    fetches[0].wait()

    @pl.when(early)
    def _():
        pl.semaphore_wait(barrier, late_from - 1)
        to_others(0, late_from, send)

    @pl.when(jnp.logical_not(early))
    def _():
        pl.semaphore_wait(barrier, n - 1)
        for d in range(late_from):
            announce(d)
        to_others(0, n, send)

    window_row = lax.broadcasted_iota(jnp.int32, (depth, LANES), 0)
    window_lane = lax.broadcasted_iota(jnp.int32, (depth, LANES), 1)
    window = ((window_row >= window_lane) & (window_row < window_lane + L)).astype(F32)
    window_ref[...] = window.astype(BF16)

    fetches[1].wait()
    band_row = lax.broadcasted_iota(jnp.int32, (LAGS, LANES), 0)
    band_lane = lax.broadcasted_iota(jnp.int32, (LAGS, LANES), 1)
    upper = band_lane >= band_row
    owner_row = lax.broadcasted_iota(jnp.int32, (own, own * LAGS), 0)
    owner_lane = lax.broadcasted_iota(jnp.int32, (own, own * LAGS), 1) // LAGS
    for c in range(NCH):
        values = templates_ref[c].astype(F32)
        mean = jnp.sum(values, axis=1, keepdims=True) / L
        centered = (values - mean).astype(BF16).astype(F32)
        power = jnp.sum(centered * centered, axis=1, keepdims=True) / L
        factor = 1.0 / (NCH * L * jnp.sqrt(power + 1e-06))
        row = jnp.sum(jnp.where(owner_row == owner_lane, factor, 0.0), axis=0, keepdims=True)
        factors_ref[c] = jnp.broadcast_to(row, (ROWS, own * LAGS))
        before = [jnp.zeros((LAGS, LANES), F32)] * own
        for k in range(wave_blocks + 1):
            if k < wave_blocks:
                turned = [
                    pltpu.roll(
                        jnp.broadcast_to(centered[t : t + 1, LANES * k : LANES * (k + 1)], (LAGS, LANES)),
                        0, 1, stride=1, stride_axis=0,
                    )
                    for t in range(own)
                ]
            else:
                turned = [jnp.zeros((LAGS, LANES), F32)] * own
            for g in range(groups):
                merged = jnp.concatenate(
                    [jnp.where(upper, turned[t], before[t]) for t in range(SUB * g, SUB * (g + 1))], axis=0
                )
                bands[c, LANES * k : LANES * (k + 1), LANES * g : LANES * (g + 1)] = merged.T.astype(BF16)
            before = turned

    @pl.when(early)
    def _():
        pl.semaphore_wait(late_sem, n - late_from)
        for d in range(late_from, n):
            send(d)

    for fetch in fetches[2:]:
        fetch.wait()
    width = counts_ref.shape[1]
    first_own = me * own

    def near(ref):
        found = ref[:, :LANES]
        for b in range(1, width // LANES):
            found = jnp.where(first_own // LANES == b, ref[:, LANES * b : LANES * (b + 1)], found)
        return found

    lists, counts, offsets = near(lists_ref), near(counts_ref), near(offsets_ref)
    station = lax.broadcasted_iota(jnp.int32, (n, LANES), 0)
    lane = lax.broadcasted_iota(jnp.int32, (n, LANES), 1)
    table = jnp.zeros((n, LANES), jnp.int32)
    for k in range(lists_ref.shape[0]):
        match = (lists[k : k + 1, :] == station) & (k < counts)
        table = table + jnp.where(match, offsets[k : k + 1, :] + 256, 0)
    here = lax.rem(first_own, LANES)
    for g in range(groups):
        for v in range(SUB):
            group = lax.bitwise_xor(lane // LAGS, v)
            code = jnp.take_along_axis(table, here + SUB * g + group, axis=1, mode="promise_in_bounds")
            sources[g, v] = LAGS * group + ((lane + code) & (LAGS - 1))
            if v == 0:
                lane_codes[g] = code

    def stage(sender):
        samples = slots[sender].astype(F32)
        for b in range(blocks):
            first_row = pl.multiple_of(sender * station_rows + ROWS * b, ROWS)
            staged[pl.ds(first_row, NCH), :] = samples[:, LANES * b : LANES * (b + 1)]

    lane = lax.broadcasted_iota(jnp.int32, (ROWS, LANES), 1)
    sub = lax.broadcasted_iota(jnp.int32, (ROWS, LANES), 0)
    inner = lane & (LAGS - 1)
    lane_group = lane // LAGS
    octets = n // ROWS
    out_parts = NTAU // LAGS
    out_blocks = NTAU // LANES
    total = [[[None] * SUB for _ in range(groups)] for _ in range(out_blocks)]

    for turn in range(octets):
        first = jnp.where(early, turn, octets - 1 - turn) * ROWS

        @pl.loop(0, ROWS)
        def receive(i):
            sender = first + i

            @pl.when(sender != me)
            def _():
                pltpu.make_async_remote_copy(
                    src_ref=slots.at[sender],
                    dst_ref=slots.at[sender],
                    send_sem=send_sem.at[sender],
                    recv_sem=recv_sem.at[sender],
                    device_id={"sta": sender},
                    device_id_type=MESH,
                ).wait_recv()

        for i in range(ROWS):
            stage(first + i)

        parts = [
            [staged[pl.ds(first * station_rows + ROWS * b + c, ROWS, stride=station_rows), :] for b in range(blocks)]
            for c in range(NCH)
        ]

        pieces = []
        for b in range(blocks):
            rows = [parts[c][b] for c in range(NCH)]
            for c in range(NCH):
                square = parts[c][b] * parts[c][b]
                high = square.astype(BF16).astype(F32)
                rows += [high, square - high]
            rows.append(rows[0])
            pieces.append(jnp.concatenate(rows, axis=0).astype(BF16))
        stacked = jnp.concatenate(
            [jnp.concatenate(pieces[b : b + wave_blocks + 1], axis=1) for b in range(lag_blocks)], axis=0
        )
        sums = jnp.dot(stacked, window_ref[...], preferred_element_type=F32)
        held = ROWS * (3 * NCH + 1)

        fitted = [[None] * groups for _ in range(parts_of_lags)]
        for c in range(NCH):
            shifted = [parts[c]]
            for j in range(1, SUB):
                rolled = [pltpu.roll(x, LANES - LAGS * j, 1) for x in parts[c]]
                stays = lane < LANES - LAGS * j
                shifted.append(
                    [jnp.where(stays, rolled[b], rolled[b + 1]) for b in range(blocks - 1)] + [rolled[-1]]
                )
            packed = [
                [jnp.concatenate([shifted[j][b], shifted[j + 1][b]], axis=0).astype(BF16) for b in range(blocks)]
                for j in range(0, SUB, 2)
            ]
            operand = jnp.concatenate(
                [
                    jnp.concatenate(packed[j][b : b + wave_blocks + 1], axis=1)
                    for b in range(lag_blocks)
                    for j in range(SUB // 2)
                ],
                axis=0,
            )
            products = jnp.dot(operand, bands[c], preferred_element_type=F32)
            for b in range(lag_blocks):
                base = held * b
                mean_one = sums[base + ROWS * c : base + ROWS * (c + 1)] / L
                at = base + ROWS * (NCH + 2 * c)
                mean_two = (sums[at : at + ROWS] + sums[at + ROWS : at + 2 * ROWS]) / L
                inverse = lax.rsqrt(mean_two - mean_one * mean_one + 1e-05)
                for j in range(SUB):
                    k = SUB * b + j
                    spread = jnp.take_along_axis(inverse, inner + LAGS * j, axis=1, mode="promise_in_bounds")
                    for g in range(groups):
                        lanes = slice(LANES * g, LANES * (g + 1))
                        term = products[ROWS * k : ROWS * (k + 1), lanes] * (spread * factors_ref[c, :, lanes])
                        fitted[k][g] = term if c == 0 else fitted[k][g] + term

        rows = pl.ds(pl.multiple_of(first, ROWS), ROWS)
        for g in range(groups):
            code = lane_codes[g, rows, :]
            far, half, member = (code & 64) != 0, (code & 32) != 0, code >= 256
            wraps = inner < (code & (LAGS - 1))
            one = [jnp.where(far, fitted[k + 2][g], fitted[k][g]) for k in range(out_parts + 2)]
            two = [jnp.where(half, one[k + 1], one[k]) for k in range(out_parts + 1)]
            picked = [
                jnp.where(member, jnp.where(wraps, two[k + 1], two[k]), 0.0) for k in range(out_parts)
            ]
            for b in range(out_blocks):
                mixed = picked[SUB * b : SUB * (b + 1)]
                for bit in (1, 2):
                    flipped = (lane_group & bit) != 0
                    mixed = [jnp.where(flipped, mixed[v ^ bit], mixed[v]) for v in range(SUB)]
                for v in range(SUB):
                    moved = jnp.take_along_axis(mixed[v], sources[g, v, rows, :], axis=1, mode="promise_in_bounds")
                    total[b][g][v] = moved if turn == 0 else total[b][g][v] + moved

    for b in range(out_blocks):
        level = [x for g in range(groups) for x in total[b][g]]
        distance = 1
        while distance < ROWS:
            low = (sub & distance) == 0
            if distance < SUB:
                low = low == ((lane_group & distance) == 0)
            level = [
                jnp.where(low, x, y) + pltpu.roll(jnp.where(low, y, x), distance, 0)
                for x, y in zip(level[::2], level[1::2])
            ]
            distance *= 2
        out_ref[:, LANES * b : LANES * (b + 1)] = level[0]

    @pl.loop(1, n)
    def sent(step):
        copy_to(lax.rem(me + step, n)).wait_send()


def body(n, data, templates, station_lists, counts, offsets):
    own, _, length = templates.shape
    operands = (data, jnp.transpose(templates, (1, 0, 2)), station_lists, counts[None, :], offsets)
    return pl.pallas_call(
        functools.partial(network_kernel, n),
        out_shape=jax.ShapeDtypeStruct((own, NTAU), F32),
        in_specs=[pl.BlockSpec(memory_space=pltpu.HBM)] * len(operands),
        out_specs=pl.BlockSpec(memory_space=pltpu.VMEM),
        scratch_shapes=[pltpu.VMEM(x.shape, x.dtype) for x in operands[1:]]
        + [
            pltpu.VMEM((n, *data.shape[1:]), data.dtype),
            pltpu.VMEM((n * ROWS * (data.shape[2] // LANES), LANES), F32),
            pltpu.VMEM((NCH, length + LANES, own * LAGS), BF16),
            pltpu.VMEM((NCH, ROWS, own * LAGS), F32),
            pltpu.VMEM((length + LANES, LANES), BF16),
            pltpu.VMEM((own // SUB, n, LANES), jnp.int32),
            pltpu.VMEM((own // SUB, SUB, n, LANES), jnp.int32),
            pltpu.SemaphoreType.DMA((len(operands),)),
            pltpu.SemaphoreType.DMA((n,)),
            pltpu.SemaphoreType.DMA((n,)),
            pltpu.SemaphoreType.REGULAR,
        ],
        compiler_params=pltpu.CompilerParams(
            collective_id=0, has_side_effects=True, vmem_limit_bytes=40 * 1024 * 1024
        ),
    )(*[pltpu.with_memory_space_constraint(x, pltpu.HBM) for x in operands])


def solution(mesh):
    placed = (P(("parts", "sta"), None, None), P("sta", None, None), P(), P(), P())
    return jax.shard_map(
        functools.partial(body, mesh.shape["sta"]), mesh=mesh, in_specs=placed,
        out_specs=P(("parts", "sta"), None), check_vma=False,
    )
```

```python
import functools

import jax
import jax.numpy as jnp
from jax import lax
from jax.experimental import pallas as pl
from jax.experimental.pallas import tpu as pltpu
from jax.sharding import PartitionSpec as P

NCH = 3
L = 512
NTAU = 256
LANES = 128
ROWS = 8
LAGS = 32
SUB = LANES // LAGS
F32 = jnp.float32
BF16 = jnp.bfloat16
MESH = pl.DeviceIdType.MESH


def network_kernel(
    n, data_hbm, templates_hbm, lists_hbm, counts_hbm, offsets_hbm, out_ref,
    templates_ref, lists_ref, counts_ref, offsets_ref,
    slots, staged, bands, factors_ref, window_ref, lane_codes, sources,
    fetch_sem, send_sem, recv_sem, late_sem,
):
    me = lax.axis_index("sta")
    fetches = [
        pltpu.make_async_copy(source, target, fetch_sem.at[i])
        for i, (source, target) in enumerate(
            [
                (data_hbm.at[0], slots.at[me]), (templates_hbm, templates_ref), (lists_hbm, lists_ref),
                (counts_hbm, counts_ref), (offsets_hbm, offsets_ref),
            ]
        )
    ]
    fetches[0].start()
    samples_len = data_hbm.shape[2]
    blocks = samples_len // LANES
    lag_blocks = (samples_len - L) // LANES
    wave_blocks = L // LANES
    own = templates_ref.shape[1]
    groups = own // SUB
    station_rows = ROWS * blocks
    parts_of_lags = lag_blocks * SUB

    late_from = n - n // 4
    early = me < late_from
    barrier = pltpu.get_barrier_semaphore()

    def others(low, high):
        return [d + jnp.where(me <= d, 1, 0).astype(jnp.int32) for d in range(low, high - 1)]

    def greet(d):
        pl.semaphore_signal(barrier, inc=1, device_id={"sta": d}, device_id_type=MESH)

    @pl.when(early)
    def _():
        for d in range(late_from, n):
            greet(jnp.int32(d))
        for d in others(0, late_from):
            greet(d)

    @pl.when(jnp.logical_not(early))
    def _():
        for d in others(late_from, n):
            greet(d)

    for fetch in fetches[1:]:
        fetch.start()

    def copy_to(target):
        return pltpu.make_async_remote_copy(
            src_ref=slots.at[me],
            dst_ref=slots.at[me],
            send_sem=send_sem,
            recv_sem=recv_sem.at[me // ROWS],
            device_id={"sta": target},
            device_id_type=MESH,
        )

    fetches[0].wait()

    @pl.when(early)
    def _():
        pl.semaphore_wait(barrier, late_from - 1)
        for d in others(0, late_from):
            copy_to(d).start()

    @pl.when(jnp.logical_not(early))
    def _():
        pl.semaphore_wait(barrier, n - 1)
        for d in range(late_from):
            copy_to(jnp.int32(d)).start()
            pl.semaphore_signal(late_sem, inc=1, device_id={"sta": jnp.int32(d)}, device_id_type=MESH)
        for d in others(late_from, n):
            copy_to(d).start()

    window_row = lax.broadcasted_iota(jnp.int32, (2 * LANES, LANES), 0)
    window_lane = lax.broadcasted_iota(jnp.int32, (2 * LANES, LANES), 1)
    window = ((window_row >= window_lane) & (window_row < window_lane + LANES)).astype(F32)
    window_ref[...] = window.astype(BF16)

    fetches[1].wait()
    band_row = lax.broadcasted_iota(jnp.int32, (LAGS, LANES), 0)
    band_lane = lax.broadcasted_iota(jnp.int32, (LAGS, LANES), 1)
    upper = band_lane >= band_row
    owner_row = lax.broadcasted_iota(jnp.int32, (own, own * LAGS), 0)
    owner_lane = lax.broadcasted_iota(jnp.int32, (own, own * LAGS), 1) // LAGS
    for c in range(NCH):
        values = templates_ref[c].astype(F32)
        mean = jnp.sum(values, axis=1, keepdims=True) / L
        centered = (values - mean).astype(BF16).astype(F32)
        power = jnp.sum(centered * centered, axis=1, keepdims=True) / L
        factor = 1.0 / (NCH * L * jnp.sqrt(power + 1e-06))
        row = jnp.sum(jnp.where(owner_row == owner_lane, factor, 0.0), axis=0, keepdims=True)
        factors_ref[c] = jnp.broadcast_to(row, (ROWS, own * LAGS))
        before = [jnp.zeros((LAGS, LANES), F32)] * own
        for k in range(wave_blocks + 1):
            if k < wave_blocks:
                turned = [
                    pltpu.roll(
                        jnp.broadcast_to(centered[t : t + 1, LANES * k : LANES * (k + 1)], (LAGS, LANES)),
                        0, 1, stride=1, stride_axis=0,
                    )
                    for t in range(own)
                ]
            else:
                turned = [jnp.zeros((LAGS, LANES), F32)] * own
            for g in range(groups):
                merged = jnp.concatenate(
                    [jnp.where(upper, turned[t], before[t]) for t in range(SUB * g, SUB * (g + 1))], axis=0
                )
                bands[c, LANES * k : LANES * (k + 1), LANES * g : LANES * (g + 1)] = merged.T.astype(BF16)
            before = turned

    @pl.when(early)
    def _():
        pl.semaphore_wait(late_sem, n - late_from)
        for d in range(late_from, n):
            copy_to(jnp.int32(d)).start()

    for fetch in fetches[2:]:
        fetch.wait()
    width = counts_ref.shape[1]
    first_own = me * own

    def near(ref):
        found = ref[:, :LANES]
        for b in range(1, width // LANES):
            found = jnp.where(first_own // LANES == b, ref[:, LANES * b : LANES * (b + 1)], found)
        return found

    lists, counts, offsets = near(lists_ref), near(counts_ref), near(offsets_ref)
    station = lax.broadcasted_iota(jnp.int32, (n, LANES), 0)
    lane = lax.broadcasted_iota(jnp.int32, (n, LANES), 1)
    table = jnp.zeros((n, LANES), jnp.int32)
    for k in range(lists_ref.shape[0]):
        match = (lists[k : k + 1, :] == station) & (k < counts)
        table = table + jnp.where(match, offsets[k : k + 1, :] + 256, 0)
    here = lax.rem(first_own, LANES)
    for g in range(groups):
        for v in range(SUB):
            group = lax.bitwise_xor(lane // LAGS, v)
            code = jnp.take_along_axis(table, here + SUB * g + group, axis=1, mode="promise_in_bounds")
            sources[g, v] = LAGS * group + ((lane + code) & (LAGS - 1))
            if v == 0:
                lane_codes[g] = code

    def arrival(semaphore, count):
        some = slots.at[pl.ds(0, count)]
        return pltpu.make_async_copy(some, some, semaphore)

    def stage(sender):
        samples = slots[sender].astype(F32)
        for b in range(blocks):
            first_row = pl.multiple_of(sender * station_rows + ROWS * b, ROWS)
            staged[pl.ds(first_row, NCH), :] = samples[:, LANES * b : LANES * (b + 1)]

    lane = lax.broadcasted_iota(jnp.int32, (ROWS, LANES), 1)
    sub = lax.broadcasted_iota(jnp.int32, (ROWS, LANES), 0)
    inner = lane & (LAGS - 1)
    lane_group = lane // LAGS
    octets = n // ROWS
    out_parts = NTAU // LAGS
    out_blocks = NTAU // LANES
    total = [[[None] * SUB for _ in range(groups)] for _ in range(out_blocks)]

    for turn in range(octets):
        first = jnp.where(early, turn, octets - 1 - turn) * ROWS

        octet = first // ROWS
        if turn == octets - 1:
            arrival(send_sem, n - 1).wait()
        pl.when(me // ROWS == octet)(arrival(recv_sem.at[octet], ROWS - 1).wait)
        pl.when(me // ROWS != octet)(arrival(recv_sem.at[octet], ROWS).wait)
        for i in range(ROWS):
            stage(first + i)

        parts = [
            [staged[pl.ds(first * station_rows + ROWS * b + c, ROWS, stride=station_rows), :] for b in range(blocks)]
            for c in range(NCH)
        ]

        squares = [[x * x for x in parts[c]] for c in range(NCH)]
        inside = [
            [
                [
                    jnp.sum(functools.reduce(jnp.add, x[b + 1 : b + wave_blocks]), axis=1, keepdims=True)
                    for x in (parts[c], squares[c])
                ]
                for b in range(lag_blocks)
            ]
            for c in range(NCH)
        ]
        pieces = []
        for b in range(blocks):
            rows = [parts[c][b] for c in range(NCH)]
            for c in range(NCH):
                square = squares[c][b]
                high = square.astype(BF16).astype(F32)
                rows += [high, square - high]
            rows.append(rows[0])
            pieces.append(jnp.concatenate(rows, axis=0).astype(BF16))
        stacked = jnp.concatenate(
            [jnp.concatenate([pieces[b], pieces[b + wave_blocks]], axis=1) for b in range(lag_blocks)], axis=0
        )
        sums = jnp.dot(stacked, window_ref[...], preferred_element_type=F32)
        held = ROWS * (3 * NCH + 1)

        fitted = [[None] * groups for _ in range(parts_of_lags)]
        for c in range(NCH):
            shifted = [parts[c]]
            for j in range(1, SUB):
                rolled = [pltpu.roll(x, LANES - LAGS * j, 1) for x in parts[c]]
                stays = lane < LANES - LAGS * j
                shifted.append(
                    [jnp.where(stays, rolled[b], rolled[b + 1]) for b in range(blocks - 1)] + [rolled[-1]]
                )
            packed = [
                [jnp.concatenate([shifted[j][b], shifted[j + 1][b]], axis=0).astype(BF16) for b in range(blocks)]
                for j in range(0, SUB, 2)
            ]
            operand = jnp.concatenate(
                [
                    jnp.concatenate(packed[j][b : b + wave_blocks + 1], axis=1)
                    for b in range(lag_blocks)
                    for j in range(SUB // 2)
                ],
                axis=0,
            )
            products = jnp.dot(operand, bands[c], preferred_element_type=F32)
            for b in range(lag_blocks):
                base = held * b
                whole, whole_squares = inside[c][b]
                mean_one = (sums[base + ROWS * c : base + ROWS * (c + 1)] + whole) / L
                at = base + ROWS * (NCH + 2 * c)
                mean_two = (sums[at : at + ROWS] + sums[at + ROWS : at + 2 * ROWS] + whole_squares) / L
                inverse = lax.rsqrt(mean_two - mean_one * mean_one + 1e-05)
                for j in range(SUB):
                    k = SUB * b + j
                    spread = jnp.take_along_axis(inverse, inner + LAGS * j, axis=1, mode="promise_in_bounds")
                    for g in range(groups):
                        lanes = slice(LANES * g, LANES * (g + 1))
                        term = products[ROWS * k : ROWS * (k + 1), lanes] * (spread * factors_ref[c, :, lanes])
                        fitted[k][g] = term if c == 0 else fitted[k][g] + term

        rows = pl.ds(pl.multiple_of(first, ROWS), ROWS)
        for g in range(groups):
            code = lane_codes[g, rows, :]
            far, half, member = (code & 64) != 0, (code & 32) != 0, code >= 256
            wraps = inner < (code & (LAGS - 1))
            one = [jnp.where(far, fitted[k + 2][g], fitted[k][g]) for k in range(out_parts + 2)]
            two = [jnp.where(half, one[k + 1], one[k]) for k in range(out_parts + 1)]
            picked = [
                jnp.where(member, jnp.where(wraps, two[k + 1], two[k]), 0.0) for k in range(out_parts)
            ]
            for b in range(out_blocks):
                mixed = picked[SUB * b : SUB * (b + 1)]
                for bit in (1, 2):
                    flipped = (lane_group & bit) != 0
                    mixed = [jnp.where(flipped, mixed[v ^ bit], mixed[v]) for v in range(SUB)]
                for v in range(SUB):
                    moved = jnp.take_along_axis(mixed[v], sources[g, v, rows, :], axis=1, mode="promise_in_bounds")
                    total[b][g][v] = moved if turn == 0 else total[b][g][v] + moved

    for b in range(out_blocks):
        level = [x for g in range(groups) for x in total[b][g]]
        distance = 1
        while distance < ROWS:
            low = (sub & distance) == 0
            if distance < SUB:
                low = low == ((lane_group & distance) == 0)
            level = [
                jnp.where(low, x, y) + pltpu.roll(jnp.where(low, y, x), distance, 0)
                for x, y in zip(level[::2], level[1::2])
            ]
            distance *= 2
        out_ref[:, LANES * b : LANES * (b + 1)] = level[0]


def body(n, data, templates, station_lists, counts, offsets):
    own, _, length = templates.shape
    operands = (data, jnp.transpose(templates, (1, 0, 2)), station_lists, counts[None, :], offsets)
    return pl.pallas_call(
        functools.partial(network_kernel, n),
        out_shape=jax.ShapeDtypeStruct((own, NTAU), F32),
        in_specs=[pl.BlockSpec(memory_space=pltpu.HBM)] * len(operands),
        out_specs=pl.BlockSpec(memory_space=pltpu.VMEM),
        scratch_shapes=[pltpu.VMEM(x.shape, x.dtype) for x in operands[1:]]
        + [
            pltpu.VMEM((n, *data.shape[1:]), data.dtype),
            pltpu.VMEM((n * ROWS * (data.shape[2] // LANES), LANES), F32),
            pltpu.VMEM((NCH, length + LANES, own * LAGS), BF16),
            pltpu.VMEM((NCH, ROWS, own * LAGS), F32),
            pltpu.VMEM((2 * LANES, LANES), BF16),
            pltpu.VMEM((own // SUB, n, LANES), jnp.int32),
            pltpu.VMEM((own // SUB, SUB, n, LANES), jnp.int32),
            pltpu.SemaphoreType.DMA((len(operands),)),
            pltpu.SemaphoreType.DMA,
            pltpu.SemaphoreType.DMA((n // ROWS,)),
            pltpu.SemaphoreType.REGULAR,
        ],
        compiler_params=pltpu.CompilerParams(
            collective_id=0, has_side_effects=True, vmem_limit_bytes=40 * 1024 * 1024
        ),
    )(*[pltpu.with_memory_space_constraint(x, pltpu.HBM) for x in operands])


def solution(mesh):
    placed = (P(("parts", "sta"), None, None), P("sta", None, None), P(), P(), P())
    return jax.shard_map(
        functools.partial(body, mesh.shape["sta"]), mesh=mesh, in_specs=placed,
        out_specs=P(("parts", "sta"), None), check_vma=False,
    )
```

```python
import functools

import jax
import jax.numpy as jnp
from jax import lax
from jax.experimental import pallas as pl
from jax.experimental.pallas import tpu as pltpu
from jax.sharding import PartitionSpec as P

NCH = 3
L = 512
NTAU = 256
LANES = 128
ROWS = 8
LAGS = 32
SUB = LANES // LAGS
F32 = jnp.float32
BF16 = jnp.bfloat16
MESH = pl.DeviceIdType.MESH


def network_kernel(
    n, data_hbm, templates_hbm, lists_hbm, counts_hbm, offsets_hbm, out_ref,
    templates_ref, lists_ref, counts_ref, offsets_ref,
    slots, staged, bands, factors_ref, window_ref, lane_codes, sources,
    fetch_sem, send_sem, recv_sem, joined, complete,
):
    me = lax.axis_index("sta")
    fetches = [
        pltpu.make_async_copy(source, target, fetch_sem.at[i])
        for i, (source, target) in enumerate(
            [
                (data_hbm.at[0], slots.at[me]), (templates_hbm, templates_ref), (lists_hbm, lists_ref),
                (counts_hbm, counts_ref), (offsets_hbm, offsets_ref),
            ]
        )
    ]
    fetches[0].start()
    samples_len = data_hbm.shape[2]
    blocks = samples_len // LANES
    lag_blocks = (samples_len - L) // LANES
    wave_blocks = L // LANES
    own = templates_ref.shape[1]
    groups = own // SUB
    station_rows = ROWS * blocks
    parts_of_lags = lag_blocks * SUB

    gap = n // 4
    late_from = n - gap
    roots = 2
    early = me < late_from
    barrier = pltpu.get_barrier_semaphore()

    def others(low, high):
        return [d + jnp.where(me <= d, 1, 0).astype(jnp.int32) for d in range(low, high - 1)]

    def tell(semaphore, d):
        pl.semaphore_signal(semaphore, inc=1, device_id={"sta": d}, device_id_type=MESH)

    direct = late_from + gap // 2

    @pl.when(me < roots)
    def _():
        for d in reversed(range(direct, n)):
            tell(barrier, jnp.int32(d))

    @pl.when(early)
    def _():
        for d in range(late_from, direct):
            tell(barrier, jnp.int32(d))
        for d in others(0, late_from):
            tell(barrier, d)

    for fetch in fetches[1:]:
        fetch.start()

    def copy_to(target, source=slots.at[me]):
        return pltpu.make_async_remote_copy(
            src_ref=source,
            dst_ref=slots.at[me],
            send_sem=send_sem,
            recv_sem=recv_sem.at[me // ROWS],
            device_id={"sta": target},
            device_id_type=MESH,
        )

    @pl.when(early)
    def _():
        fetches[0].wait()
        pl.semaphore_wait(barrier, late_from - 1)

        @pl.when((me + gap >= direct) & (me + gap < n))
        def _():
            tell(barrier, me + gap)

        for d in others(0, late_from):
            copy_to(d).start()

    @pl.when(jnp.logical_not(early))
    def _():
        @pl.when(me < direct)
        def _():
            fetches[0].wait()
            pl.semaphore_wait(barrier, late_from)
            for d in range(late_from):
                copy_to(jnp.int32(d)).start()
                tell(joined, jnp.int32(d))

        @pl.when(me >= direct)
        def _():
            pl.semaphore_wait(barrier, roots)
            for d in range(roots):
                copy_to(jnp.int32(d), data_hbm.at[0]).start()
                tell(joined, jnp.int32(d))
            fetches[0].wait()
            pl.semaphore_wait(barrier, 1)
            for d in range(roots, late_from):
                tell(joined, jnp.int32(d))
                copy_to(jnp.int32(d)).start()

    window_row = lax.broadcasted_iota(jnp.int32, (2 * LANES, LANES), 0)
    window_lane = lax.broadcasted_iota(jnp.int32, (2 * LANES, LANES), 1)
    window = ((window_row >= window_lane) & (window_row < window_lane + LANES)).astype(F32)
    window_ref[...] = window.astype(BF16)

    fetches[1].wait()
    band_row = lax.broadcasted_iota(jnp.int32, (LAGS, LANES), 0)
    band_lane = lax.broadcasted_iota(jnp.int32, (LAGS, LANES), 1)
    upper = band_lane >= band_row
    owner_row = lax.broadcasted_iota(jnp.int32, (own, own * LAGS), 0)
    owner_lane = lax.broadcasted_iota(jnp.int32, (own, own * LAGS), 1) // LAGS
    for c in range(NCH):
        values = templates_ref[c].astype(F32)
        mean = jnp.sum(values, axis=1, keepdims=True) / L
        centered = (values - mean).astype(BF16).astype(F32)
        power = jnp.sum(centered * centered, axis=1, keepdims=True) / L
        factor = 1.0 / (NCH * L * jnp.sqrt(power + 1e-06))
        row = jnp.sum(jnp.where(owner_row == owner_lane, factor, 0.0), axis=0, keepdims=True)
        factors_ref[c] = jnp.broadcast_to(row, (ROWS, own * LAGS))
        before = [jnp.zeros((LAGS, LANES), F32)] * own
        for k in range(wave_blocks + 1):
            if k < wave_blocks:
                turned = [
                    pltpu.roll(
                        jnp.broadcast_to(centered[t : t + 1, LANES * k : LANES * (k + 1)], (LAGS, LANES)),
                        0, 1, stride=1, stride_axis=0,
                    )
                    for t in range(own)
                ]
            else:
                turned = [jnp.zeros((LAGS, LANES), F32)] * own
            for g in range(groups):
                merged = jnp.concatenate(
                    [jnp.where(upper, turned[t], before[t]) for t in range(SUB * g, SUB * (g + 1))], axis=0
                )
                bands[c, LANES * k : LANES * (k + 1), LANES * g : LANES * (g + 1)] = merged.T.astype(BF16)
            before = turned

    @pl.when(early)
    def _():
        pl.semaphore_wait(joined, n - late_from)

        @pl.when(me >= late_from - gap)
        def _():
            tell(complete, me + gap)

        for d in range(late_from, n):
            copy_to(jnp.int32(d)).start()

    @pl.when(jnp.logical_not(early))
    def _():
        pl.semaphore_wait(complete, 1)
        for d in others(late_from, n):
            copy_to(d).start()

    for fetch in fetches[2:]:
        fetch.wait()
    width = counts_ref.shape[1]
    first_own = me * own

    def near(ref):
        found = ref[:, :LANES]
        for b in range(1, width // LANES):
            found = jnp.where(first_own // LANES == b, ref[:, LANES * b : LANES * (b + 1)], found)
        return found

    lists, counts, offsets = near(lists_ref), near(counts_ref), near(offsets_ref)
    station = lax.broadcasted_iota(jnp.int32, (n, LANES), 0)
    lane = lax.broadcasted_iota(jnp.int32, (n, LANES), 1)
    table = jnp.zeros((n, LANES), jnp.int32)
    for k in range(lists_ref.shape[0]):
        match = (lists[k : k + 1, :] == station) & (k < counts)
        table = table + jnp.where(match, offsets[k : k + 1, :] + 256, 0)
    here = lax.rem(first_own, LANES)
    for g in range(groups):
        for v in range(SUB):
            group = lax.bitwise_xor(lane // LAGS, v)
            code = jnp.take_along_axis(table, here + SUB * g + group, axis=1, mode="promise_in_bounds")
            sources[g, v] = LAGS * group + ((lane + code) & (LAGS - 1))
            if v == 0:
                lane_codes[g] = code

    def arrival(semaphore, count):
        some = slots.at[pl.ds(0, count)]
        return pltpu.make_async_copy(some, some, semaphore)

    def stage(sender):
        samples = slots[sender].astype(F32)
        for b in range(blocks):
            first_row = pl.multiple_of(sender * station_rows + ROWS * b, ROWS)
            staged[pl.ds(first_row, NCH), :] = samples[:, LANES * b : LANES * (b + 1)]

    lane = lax.broadcasted_iota(jnp.int32, (ROWS, LANES), 1)
    sub = lax.broadcasted_iota(jnp.int32, (ROWS, LANES), 0)
    inner = lane & (LAGS - 1)
    lane_group = lane // LAGS
    octets = n // ROWS
    out_parts = NTAU // LAGS
    out_blocks = NTAU // LANES
    total = [[[None] * SUB for _ in range(groups)] for _ in range(out_blocks)]

    for turn in range(octets):
        first = jnp.where(early, turn, octets - 1 - turn) * ROWS

        octet = first // ROWS
        if turn == octets - 1:
            arrival(send_sem, n - 1).wait()
        pl.when(me // ROWS == octet)(arrival(recv_sem.at[octet], ROWS - 1).wait)
        pl.when(me // ROWS != octet)(arrival(recv_sem.at[octet], ROWS).wait)
        for i in range(ROWS):
            stage(first + i)

        parts = [
            [staged[pl.ds(first * station_rows + ROWS * b + c, ROWS, stride=station_rows), :] for b in range(blocks)]
            for c in range(NCH)
        ]

        squares = [[x * x for x in parts[c]] for c in range(NCH)]
        inside = [
            [
                [
                    jnp.sum(functools.reduce(jnp.add, x[b + 1 : b + wave_blocks]), axis=1, keepdims=True)
                    for x in (parts[c], squares[c])
                ]
                for b in range(lag_blocks)
            ]
            for c in range(NCH)
        ]
        pieces = []
        for b in range(blocks):
            rows = [parts[c][b] for c in range(NCH)]
            for c in range(NCH):
                square = squares[c][b]
                high = square.astype(BF16).astype(F32)
                rows += [high, square - high]
            rows.append(rows[0])
            pieces.append(jnp.concatenate(rows, axis=0).astype(BF16))
        stacked = jnp.concatenate(
            [jnp.concatenate([pieces[b], pieces[b + wave_blocks]], axis=1) for b in range(lag_blocks)], axis=0
        )
        sums = jnp.dot(stacked, window_ref[...], preferred_element_type=F32)
        held = ROWS * (3 * NCH + 1)

        fitted = [[None] * groups for _ in range(parts_of_lags)]
        for c in range(NCH):
            shifted = [parts[c]]
            for j in range(1, SUB):
                rolled = [pltpu.roll(x, LANES - LAGS * j, 1) for x in parts[c]]
                stays = lane < LANES - LAGS * j
                shifted.append(
                    [jnp.where(stays, rolled[b], rolled[b + 1]) for b in range(blocks - 1)] + [rolled[-1]]
                )
            packed = [
                [jnp.concatenate([shifted[j][b], shifted[j + 1][b]], axis=0).astype(BF16) for b in range(blocks)]
                for j in range(0, SUB, 2)
            ]
            operand = jnp.concatenate(
                [
                    jnp.concatenate(packed[j][b : b + wave_blocks + 1], axis=1)
                    for b in range(lag_blocks)
                    for j in range(SUB // 2)
                ],
                axis=0,
            )
            products = jnp.dot(operand, bands[c], preferred_element_type=F32)
            for b in range(lag_blocks):
                base = held * b
                whole, whole_squares = inside[c][b]
                mean_one = (sums[base + ROWS * c : base + ROWS * (c + 1)] + whole) / L
                at = base + ROWS * (NCH + 2 * c)
                mean_two = (sums[at : at + ROWS] + sums[at + ROWS : at + 2 * ROWS] + whole_squares) / L
                inverse = lax.rsqrt(mean_two - mean_one * mean_one + 1e-05)
                for j in range(SUB):
                    k = SUB * b + j
                    spread = jnp.take_along_axis(inverse, inner + LAGS * j, axis=1, mode="promise_in_bounds")
                    for g in range(groups):
                        lanes = slice(LANES * g, LANES * (g + 1))
                        term = products[ROWS * k : ROWS * (k + 1), lanes] * (spread * factors_ref[c, :, lanes])
                        fitted[k][g] = term if c == 0 else fitted[k][g] + term

        rows = pl.ds(pl.multiple_of(first, ROWS), ROWS)
        for g in range(groups):
            code = lane_codes[g, rows, :]
            far, half, member = (code & 64) != 0, (code & 32) != 0, code >= 256
            wraps = inner < (code & (LAGS - 1))
            one = [jnp.where(far, fitted[k + 2][g], fitted[k][g]) for k in range(out_parts + 2)]
            two = [jnp.where(half, one[k + 1], one[k]) for k in range(out_parts + 1)]
            picked = [
                jnp.where(member, jnp.where(wraps, two[k + 1], two[k]), 0.0) for k in range(out_parts)
            ]
            for b in range(out_blocks):
                mixed = picked[SUB * b : SUB * (b + 1)]
                for bit in (1, 2):
                    flipped = (lane_group & bit) != 0
                    mixed = [jnp.where(flipped, mixed[v ^ bit], mixed[v]) for v in range(SUB)]
                for v in range(SUB):
                    moved = jnp.take_along_axis(mixed[v], sources[g, v, rows, :], axis=1, mode="promise_in_bounds")
                    total[b][g][v] = moved if turn == 0 else total[b][g][v] + moved

    for b in range(out_blocks):
        level = [x for g in range(groups) for x in total[b][g]]
        distance = 1
        while distance < ROWS:
            low = (sub & distance) == 0
            if distance < SUB:
                low = low == ((lane_group & distance) == 0)
            level = [
                jnp.where(low, x, y) + pltpu.roll(jnp.where(low, y, x), distance, 0)
                for x, y in zip(level[::2], level[1::2])
            ]
            distance *= 2
        out_ref[:, LANES * b : LANES * (b + 1)] = level[0]


def body(n, data, templates, station_lists, counts, offsets):
    own, _, length = templates.shape
    operands = (data, jnp.transpose(templates, (1, 0, 2)), station_lists, counts[None, :], offsets)
    return pl.pallas_call(
        functools.partial(network_kernel, n),
        out_shape=jax.ShapeDtypeStruct((own, NTAU), F32),
        in_specs=[pl.BlockSpec(memory_space=pltpu.HBM)] * len(operands),
        out_specs=pl.BlockSpec(memory_space=pltpu.VMEM),
        scratch_shapes=[pltpu.VMEM(x.shape, x.dtype) for x in operands[1:]]
        + [
            pltpu.VMEM((n, *data.shape[1:]), data.dtype),
            pltpu.VMEM((n * ROWS * (data.shape[2] // LANES), LANES), F32),
            pltpu.VMEM((NCH, length + LANES, own * LAGS), BF16),
            pltpu.VMEM((NCH, ROWS, own * LAGS), F32),
            pltpu.VMEM((2 * LANES, LANES), BF16),
            pltpu.VMEM((own // SUB, n, LANES), jnp.int32),
            pltpu.VMEM((own // SUB, SUB, n, LANES), jnp.int32),
            pltpu.SemaphoreType.DMA((len(operands),)),
            pltpu.SemaphoreType.DMA,
            pltpu.SemaphoreType.DMA((n // ROWS,)),
            pltpu.SemaphoreType.REGULAR,
            pltpu.SemaphoreType.REGULAR,
        ],
        compiler_params=pltpu.CompilerParams(
            collective_id=0, has_side_effects=True, vmem_limit_bytes=40 * 1024 * 1024
        ),
    )(*[pltpu.with_memory_space_constraint(x, pltpu.HBM) for x in operands])


def solution(mesh):
    placed = (P(("parts", "sta"), None, None), P("sta", None, None), P(), P(), P())
    return jax.shard_map(
        functools.partial(body, mesh.shape["sta"]), mesh=mesh, in_specs=placed,
        out_specs=P(("parts", "sta"), None), check_vma=False,
    )
```

```python
import functools

import jax
import jax.numpy as jnp
from jax import lax
from jax.experimental import pallas as pl
from jax.experimental.pallas import tpu as pltpu
from jax.sharding import PartitionSpec as P

NCH = 3
L = 512
NTAU = 256
LANES = 128
ROWS = 8
LAGS = 32
SUB = LANES // LAGS
F32 = jnp.float32
BF16 = jnp.bfloat16
MESH = pl.DeviceIdType.MESH


def network_kernel(
    n, data_hbm, templates_hbm, lists_hbm, counts_hbm, offsets_hbm, out_ref,
    templates_ref, lists_ref, counts_ref, offsets_ref,
    slots, staged, bands, factors_ref, window_ref, lane_codes, sources, totals,
    fetch_sem, send_sem, recv_sem, joined, complete,
):
    me = lax.axis_index("sta")
    fetches = [
        pltpu.make_async_copy(source, target, fetch_sem.at[i])
        for i, (source, target) in enumerate(
            [
                (data_hbm.at[0], slots.at[me]), (templates_hbm, templates_ref), (lists_hbm, lists_ref),
                (counts_hbm, counts_ref), (offsets_hbm, offsets_ref),
            ]
        )
    ]
    samples_len = data_hbm.shape[2]
    blocks = samples_len // LANES
    lag_blocks = (samples_len - L) // LANES
    wave_blocks = L // LANES
    own = templates_ref.shape[1]
    groups = own // SUB
    station_rows = ROWS * blocks
    parts_of_lags = lag_blocks * SUB

    gap = n // 4
    late_from = n - gap
    roots = 2
    early = me < late_from
    barrier = pltpu.get_barrier_semaphore()

    def others(low, high):
        return [d + jnp.where(me <= d, 1, 0).astype(jnp.int32) for d in range(low, high - 1)]

    def tell(semaphore, d):
        pl.semaphore_signal(semaphore, inc=1, device_id={"sta": d}, device_id_type=MESH)

    direct = late_from + gap // 2
    far_from = late_from - gap

    @pl.when(me < roots)
    def _():
        for d in reversed(range(direct, n)):
            tell(barrier, jnp.int32(d))

    def copy_to(target, source=slots.at[me]):
        return pltpu.make_async_remote_copy(
            src_ref=source,
            dst_ref=slots.at[me],
            send_sem=send_sem,
            recv_sem=recv_sem.at[me // ROWS],
            device_id={"sta": target},
            device_id_type=MESH,
        )

    @pl.when(me >= direct)
    def _():
        pl.semaphore_wait(barrier, roots)
        for d in range(roots):
            copy_to(jnp.int32(d), data_hbm.at[0]).start()
            tell(joined.at[1], jnp.int32(d))

    fetches[0].start()

    @pl.when(early)
    def _():
        for d in range(late_from, direct):
            tell(barrier, jnp.int32(d))
        for d in others(0, late_from):
            tell(barrier, d)

    for fetch in fetches[1:]:
        fetch.start()

    @pl.when(early)
    def _():
        fetches[0].wait()
        pl.semaphore_wait(barrier, late_from - 1)

        @pl.when((me + gap >= direct) & (me + gap < n))
        def _():
            tell(barrier, me + gap)

        @pl.when(me < far_from)
        def _():
            for d in others(0, late_from):
                copy_to(d).start()

        @pl.when(me >= far_from)
        def _():
            for d in range(roots):
                copy_to(jnp.int32(d)).start()
            for d in others(far_from, late_from):
                copy_to(d).start()

    @pl.when(jnp.logical_not(early))
    def _():
        @pl.when(me < direct)
        def _():
            fetches[0].wait()
            pl.semaphore_wait(barrier, late_from)
            for d in range(late_from):
                tell(joined.at[0], jnp.int32(d))
                if d < roots:
                    copy_to(jnp.int32(d)).start()

        @pl.when(me >= direct)
        def _():
            fetches[0].wait()
            pl.semaphore_wait(barrier, 1)
            for d in range(roots, late_from):
                tell(joined.at[1], jnp.int32(d))
                copy_to(jnp.int32(d)).start()

    window_row = lax.broadcasted_iota(jnp.int32, (2 * LANES, LANES), 0)
    window_lane = lax.broadcasted_iota(jnp.int32, (2 * LANES, LANES), 1)
    window = ((window_row >= window_lane) & (window_row < window_lane + LANES)).astype(F32)
    window_ref[...] = window.astype(BF16)

    fetches[1].wait()
    band_row = lax.broadcasted_iota(jnp.int32, (LAGS, LANES), 0)
    band_lane = lax.broadcasted_iota(jnp.int32, (LAGS, LANES), 1)
    upper = band_lane >= band_row
    owner_row = lax.broadcasted_iota(jnp.int32, (own, own * LAGS), 0)
    owner_lane = lax.broadcasted_iota(jnp.int32, (own, own * LAGS), 1) // LAGS
    for c in range(NCH):
        values = templates_ref[c].astype(F32)
        mean = jnp.sum(values, axis=1, keepdims=True) / L
        centered = (values - mean).astype(BF16).astype(F32)
        power = jnp.sum(centered * centered, axis=1, keepdims=True) / L
        factor = 1.0 / (NCH * L * jnp.sqrt(power + 1e-06))
        row = jnp.sum(jnp.where(owner_row == owner_lane, factor, 0.0), axis=0, keepdims=True)
        factors_ref[c] = jnp.broadcast_to(row, (ROWS, own * LAGS))
        before = [jnp.zeros((LAGS, LANES), F32)] * own
        for k in range(wave_blocks + 1):
            if k < wave_blocks:
                turned = [
                    pltpu.roll(
                        jnp.broadcast_to(centered[t : t + 1, LANES * k : LANES * (k + 1)], (LAGS, LANES)),
                        0, 1, stride=1, stride_axis=0,
                    )
                    for t in range(own)
                ]
            else:
                turned = [jnp.zeros((LAGS, LANES), F32)] * own
            for g in range(groups):
                merged = jnp.concatenate(
                    [jnp.where(upper, turned[t], before[t]) for t in range(SUB * g, SUB * (g + 1))], axis=0
                )
                bands[c, LANES * k : LANES * (k + 1), LANES * g : LANES * (g + 1)] = merged.T.astype(BF16)
            before = turned

    @pl.when(early)
    def _():
        @pl.when(me >= far_from)
        def _():
            for d in range(roots, far_from):
                copy_to(jnp.int32(d)).start()

        pl.semaphore_wait(joined.at[0], direct - late_from)
        for d in reversed(range(late_from, direct)):
            copy_to(jnp.int32(d)).start()

    @pl.when(early)
    def _():
        pl.semaphore_wait(joined.at[1], n - direct)

        @pl.when(me >= far_from)
        def _():
            tell(complete, me + gap)

        for d in range(direct, n):
            copy_to(jnp.int32(d)).start()

    @pl.when(jnp.logical_not(early))
    def _():
        @pl.when(me < direct)
        def _():
            for d in range(roots, late_from):
                copy_to(jnp.int32(d)).start()

        pl.semaphore_wait(complete, 1)
        for d in others(late_from, n):
            copy_to(d).start()

    for fetch in fetches[2:]:
        fetch.wait()
    width = counts_ref.shape[1]
    first_own = me * own

    def near(ref):
        found = ref[:, :LANES]
        for b in range(1, width // LANES):
            found = jnp.where(first_own // LANES == b, ref[:, LANES * b : LANES * (b + 1)], found)
        return found

    lists, counts, offsets = near(lists_ref), near(counts_ref), near(offsets_ref)
    station = lax.broadcasted_iota(jnp.int32, (n, LANES), 0)
    lane = lax.broadcasted_iota(jnp.int32, (n, LANES), 1)
    table = jnp.zeros((n, LANES), jnp.int32)
    for k in range(lists_ref.shape[0]):
        match = (lists[k : k + 1, :] == station) & (k < counts)
        table = table + jnp.where(match, offsets[k : k + 1, :] + 256, 0)
    here = lax.rem(first_own, LANES)
    for g in range(groups):
        for v in range(SUB):
            group = lax.bitwise_xor(lane // LAGS, v)
            code = jnp.take_along_axis(table, here + SUB * g + group, axis=1, mode="promise_in_bounds")
            sources[g, v] = LAGS * group + ((lane + code) & (LAGS - 1))
            if v == 0:
                lane_codes[g] = code

    def arrival(semaphore, count):
        some = slots.at[pl.ds(0, count)]
        return pltpu.make_async_copy(some, some, semaphore)

    def stage(sender):
        samples = slots[sender].astype(F32)
        for b in range(blocks):
            first_row = pl.multiple_of(sender * station_rows + ROWS * b, ROWS)
            staged[pl.ds(first_row, NCH), :] = samples[:, LANES * b : LANES * (b + 1)]

    lane = lax.broadcasted_iota(jnp.int32, (ROWS, LANES), 1)
    sub = lax.broadcasted_iota(jnp.int32, (ROWS, LANES), 0)
    inner = lane & (LAGS - 1)
    lane_group = lane // LAGS
    octets = n // ROWS
    out_parts = NTAU // LAGS
    out_blocks = NTAU // LANES

    totals[...] = jnp.zeros_like(totals)

    @pl.loop(0, octets)
    def work_off(turn):
        first = jnp.where(early, turn, octets - 1 - turn) * ROWS

        octet = first // ROWS
        here_rows = pl.ds(pl.multiple_of(first, ROWS), ROWS)
        masked = [
            [
                jnp.where(lane_codes[g, here_rows, :] >= 256, factors_ref[c, :, LANES * g : LANES * (g + 1)], 0.0)
                for g in range(groups)
            ]
            for c in range(NCH)
        ]
        pl.when(me // ROWS == octet)(arrival(recv_sem.at[octet], ROWS - 1).wait)
        pl.when(me // ROWS != octet)(arrival(recv_sem.at[octet], ROWS).wait)
        for i in range(ROWS):
            stage(first + i)

        parts = [
            [staged[pl.ds(first * station_rows + ROWS * b + c, ROWS, stride=station_rows), :] for b in range(blocks)]
            for c in range(NCH)
        ]

        squares = [[x * x for x in parts[c]] for c in range(NCH)]
        inside = [
            [
                [
                    jnp.sum(functools.reduce(jnp.add, x[b + 1 : b + wave_blocks]), axis=1, keepdims=True)
                    for x in (parts[c], squares[c])
                ]
                for b in range(lag_blocks)
            ]
            for c in range(NCH)
        ]
        pieces = []
        for b in range(blocks):
            rows = [parts[c][b] for c in range(NCH)]
            for c in range(NCH):
                square = squares[c][b]
                high = square.astype(BF16).astype(F32)
                rows += [high, square - high]
            rows.append(rows[0])
            pieces.append(jnp.concatenate(rows, axis=0).astype(BF16))
        stacked = jnp.concatenate(
            [jnp.concatenate([pieces[b], pieces[b + wave_blocks]], axis=1) for b in range(lag_blocks)], axis=0
        )
        sums = jnp.dot(stacked, window_ref[...], preferred_element_type=F32)
        held = ROWS * (3 * NCH + 1)

        inverses = [[] for _ in range(NCH)]
        for c in range(NCH):
            for b in range(lag_blocks):
                base = held * b
                whole, whole_squares = inside[c][b]
                mean_one = (sums[base + ROWS * c : base + ROWS * (c + 1)] + whole) / L
                at = base + ROWS * (NCH + 2 * c)
                mean_two = (sums[at : at + ROWS] + sums[at + ROWS : at + 2 * ROWS] + whole_squares) / L
                inverses[c].append(lax.rsqrt(mean_two - mean_one * mean_one + 1e-05))

        fitted = [[None] * groups for _ in range(parts_of_lags)]
        for c in range(NCH):
            shifted = [parts[c]]
            for j in range(1, SUB):
                rolled = [pltpu.roll(x, LANES - LAGS * j, 1) for x in parts[c]]
                stays = lane < LANES - LAGS * j
                shifted.append(
                    [jnp.where(stays, rolled[b], rolled[b + 1]) for b in range(blocks - 1)] + [rolled[-1]]
                )
            packed = [
                [jnp.concatenate([shifted[j][b], shifted[j + 1][b]], axis=0).astype(BF16) for b in range(blocks)]
                for j in range(0, SUB, 2)
            ]
            operand = jnp.concatenate(
                [
                    jnp.concatenate(packed[j][b : b + wave_blocks + 1], axis=1)
                    for b in range(lag_blocks)
                    for j in range(SUB // 2)
                ],
                axis=0,
            )
            products = jnp.dot(operand, bands[c], preferred_element_type=F32)
            for b in range(lag_blocks):
                inverse = inverses[c][b]
                for j in range(SUB):
                    k = SUB * b + j
                    spread = jnp.take_along_axis(inverse, inner + LAGS * j, axis=1, mode="promise_in_bounds")
                    for g in range(groups):
                        lanes = slice(LANES * g, LANES * (g + 1))
                        term = products[ROWS * k : ROWS * (k + 1), lanes] * (spread * masked[c][g])
                        fitted[k][g] = term if c == 0 else fitted[k][g] + term

        for g in range(groups):
            code = lane_codes[g, here_rows, :]
            far, half = (code & 64) != 0, (code & 32) != 0
            wraps = inner < (code & (LAGS - 1))
            one = [jnp.where(far, fitted[k + 2][g], fitted[k][g]) for k in range(out_parts + 2)]
            two = [jnp.where(half, one[k + 1], one[k]) for k in range(out_parts + 1)]
            picked = [jnp.where(wraps, two[k + 1], two[k]) for k in range(out_parts)]
            for b in range(out_blocks):
                mixed = picked[SUB * b : SUB * (b + 1)]
                for bit in (1, 2):
                    flipped = (lane_group & bit) != 0
                    mixed = [jnp.where(flipped, mixed[v ^ bit], mixed[v]) for v in range(SUB)]
                for v in range(SUB):
                    moved = jnp.take_along_axis(mixed[v], sources[g, v, here_rows, :], axis=1, mode="promise_in_bounds")
                    totals[b, g, v] += moved

    arrival(send_sem, n - 1).wait()

    for b in range(out_blocks):
        level = [totals[b, g, v] for g in range(groups) for v in range(SUB)]
        distance = 1
        while distance < ROWS:
            low = (sub & distance) == 0
            if distance < SUB:
                low = low == ((lane_group & distance) == 0)
            level = [
                jnp.where(low, x, y) + pltpu.roll(jnp.where(low, y, x), distance, 0)
                for x, y in zip(level[::2], level[1::2])
            ]
            distance *= 2
        out_ref[:, LANES * b : LANES * (b + 1)] = level[0]


def body(n, data, templates, station_lists, counts, offsets):
    own, _, length = templates.shape
    operands = (data, jnp.transpose(templates, (1, 0, 2)), station_lists, counts[None, :], offsets)
    return pl.pallas_call(
        functools.partial(network_kernel, n),
        out_shape=jax.ShapeDtypeStruct((own, NTAU), F32),
        in_specs=[pl.BlockSpec(memory_space=pltpu.HBM)] * len(operands),
        out_specs=pl.BlockSpec(memory_space=pltpu.VMEM),
        scratch_shapes=[pltpu.VMEM(x.shape, x.dtype) for x in operands[1:]]
        + [
            pltpu.VMEM((n, *data.shape[1:]), data.dtype),
            pltpu.VMEM((n * ROWS * (data.shape[2] // LANES), LANES), F32),
            pltpu.VMEM((NCH, length + LANES, own * LAGS), BF16),
            pltpu.VMEM((NCH, ROWS, own * LAGS), F32),
            pltpu.VMEM((2 * LANES, LANES), BF16),
            pltpu.VMEM((own // SUB, n, LANES), jnp.int32),
            pltpu.VMEM((own // SUB, SUB, n, LANES), jnp.int32),
            pltpu.VMEM((NTAU // LANES, own // SUB, SUB, ROWS, LANES), F32),
            pltpu.SemaphoreType.DMA((len(operands),)),
            pltpu.SemaphoreType.DMA,
            pltpu.SemaphoreType.DMA((n // ROWS,)),
            pltpu.SemaphoreType.REGULAR((2,)),
            pltpu.SemaphoreType.REGULAR,
        ],
        compiler_params=pltpu.CompilerParams(
            collective_id=0, has_side_effects=True, vmem_limit_bytes=40 * 1024 * 1024
        ),
    )(*[pltpu.with_memory_space_constraint(x, pltpu.HBM) for x in operands])


def solution(mesh):
    placed = (P(("parts", "sta"), None, None), P("sta", None, None), P(), P(), P())
    return jax.shard_map(
        functools.partial(body, mesh.shape["sta"]), mesh=mesh, in_specs=placed,
        out_specs=P(("parts", "sta"), None), check_vma=False,
    )
```

```python
import functools

import jax
import jax.numpy as jnp
from jax import lax
from jax.experimental import pallas as pl
from jax.experimental.pallas import tpu as pltpu
from jax.sharding import PartitionSpec as P

NCH = 3
L = 512
NTAU = 256
LANES = 128
ROWS = 8
LAGS = 32
SUB = LANES // LAGS
F32 = jnp.float32
BF16 = jnp.bfloat16
MESH = pl.DeviceIdType.MESH


def network_kernel(
    n, data_hbm, templates_hbm, lists_hbm, counts_hbm, offsets_hbm, out_ref,
    templates_ref, lists_ref, counts_ref, offsets_ref,
    slots, staged, bands, factors_ref, window_ref, lane_codes, sources, totals,
    fetch_sem, send_sem, recv_sem, joined, complete,
):
    me = lax.axis_index("sta")
    fetches = [
        pltpu.make_async_copy(source, target, fetch_sem.at[i])
        for i, (source, target) in enumerate(
            [
                (data_hbm.at[0], slots.at[me]), (templates_hbm, templates_ref), (lists_hbm, lists_ref),
                (counts_hbm, counts_ref), (offsets_hbm, offsets_ref),
            ]
        )
    ]
    samples_len = data_hbm.shape[2]
    blocks = samples_len // LANES
    lag_blocks = (samples_len - L) // LANES
    wave_blocks = L // LANES
    own = templates_ref.shape[1]
    groups = own // SUB
    station_rows = ROWS * blocks
    parts_of_lags = lag_blocks * SUB

    gap = n // 4
    late_from = n - gap
    roots = 2
    early = me < late_from
    barrier = pltpu.get_barrier_semaphore()

    def others(low, high):
        return [d + jnp.where(me <= d, 1, 0).astype(jnp.int32) for d in range(low, high - 1)]

    def tell(semaphore, d):
        pl.semaphore_signal(semaphore, inc=1, device_id={"sta": d}, device_id_type=MESH)

    direct = late_from + gap // 2
    far_from = late_from - gap

    @pl.when(me < roots)
    def _():
        for d in reversed(range(direct, n)):
            tell(barrier, jnp.int32(d))

    def copy_to(target, source=slots.at[me]):
        return pltpu.make_async_remote_copy(
            src_ref=source,
            dst_ref=slots.at[me],
            send_sem=send_sem,
            recv_sem=recv_sem.at[me // ROWS],
            device_id={"sta": target},
            device_id_type=MESH,
        )

    @pl.when(me >= direct)
    def _():
        pl.semaphore_wait(barrier, roots)
        for d in range(roots):
            copy_to(jnp.int32(d), data_hbm.at[0]).start()
            tell(joined.at[1], jnp.int32(d))

    fetches[0].start()

    @pl.when(early)
    def _():
        for d in range(late_from, direct):
            tell(barrier, jnp.int32(d))
        for d in others(0, late_from):
            tell(barrier, d)

    for fetch in fetches[1:]:
        fetch.start()

    @pl.when(early)
    def _():
        fetches[0].wait()
        pl.semaphore_wait(barrier, late_from - 1)

        @pl.when((me + gap >= direct) & (me + gap < n))
        def _():
            tell(barrier, me + gap)

        @pl.when(me < far_from)
        def _():
            for d in others(0, late_from):
                copy_to(d).start()

        @pl.when(me >= far_from)
        def _():
            for d in range(roots):
                copy_to(jnp.int32(d)).start()
            for d in others(far_from, late_from):
                copy_to(d).start()

    @pl.when(jnp.logical_not(early))
    def _():
        @pl.when(me < direct)
        def _():
            fetches[0].wait()
            pl.semaphore_wait(barrier, late_from)
            for d in range(late_from):
                tell(joined.at[0], jnp.int32(d))
                if d < roots:
                    copy_to(jnp.int32(d)).start()

        @pl.when(me >= direct)
        def _():
            fetches[0].wait()
            pl.semaphore_wait(barrier, 1)
            for d in range(roots, late_from):
                tell(joined.at[1], jnp.int32(d))

    window_row = lax.broadcasted_iota(jnp.int32, (2 * LANES, LANES), 0)
    window_lane = lax.broadcasted_iota(jnp.int32, (2 * LANES, LANES), 1)
    window = ((window_row >= window_lane) & (window_row < window_lane + LANES)).astype(F32)
    window_ref[...] = window.astype(BF16)

    fetches[1].wait()
    band_row = lax.broadcasted_iota(jnp.int32, (LAGS, LANES), 0)
    band_lane = lax.broadcasted_iota(jnp.int32, (LAGS, LANES), 1)
    upper = band_lane >= band_row
    owner_row = lax.broadcasted_iota(jnp.int32, (own, own * LAGS), 0)
    owner_lane = lax.broadcasted_iota(jnp.int32, (own, own * LAGS), 1) // LAGS
    for c in range(NCH):
        values = templates_ref[c].astype(F32)
        mean = jnp.sum(values, axis=1, keepdims=True) / L
        centered = (values - mean).astype(BF16).astype(F32)
        power = jnp.sum(centered * centered, axis=1, keepdims=True) / L
        factor = 1.0 / (NCH * L * jnp.sqrt(power + 1e-06))
        row = jnp.sum(jnp.where(owner_row == owner_lane, factor, 0.0), axis=0, keepdims=True)
        factors_ref[c] = jnp.broadcast_to(row, (ROWS, own * LAGS))
        before = [jnp.zeros((LAGS, LANES), F32)] * own
        for k in range(wave_blocks + 1):
            if k < wave_blocks:
                turned = [
                    pltpu.roll(
                        jnp.broadcast_to(centered[t : t + 1, LANES * k : LANES * (k + 1)], (LAGS, LANES)),
                        0, 1, stride=1, stride_axis=0,
                    )
                    for t in range(own)
                ]
            else:
                turned = [jnp.zeros((LAGS, LANES), F32)] * own
            for g in range(groups):
                merged = jnp.concatenate(
                    [jnp.where(upper, turned[t], before[t]) for t in range(SUB * g, SUB * (g + 1))], axis=0
                )
                bands[c, LANES * k : LANES * (k + 1), LANES * g : LANES * (g + 1)] = merged.T.astype(BF16)
            before = turned

    @pl.when(early)
    def _():
        @pl.when(me >= far_from)
        def _():
            for d in range(roots, far_from):
                copy_to(jnp.int32(d)).start()

        pl.semaphore_wait(joined.at[0], direct - late_from)
        for d in reversed(range(late_from, direct)):
            copy_to(jnp.int32(d)).start()

    @pl.when(early)
    def _():
        pl.semaphore_wait(joined.at[1], n - direct)

        @pl.when(me >= far_from)
        def _():
            tell(complete, me + gap)

        for d in range(direct, n):
            copy_to(jnp.int32(d)).start()

    @pl.when(jnp.logical_not(early))
    def _():
        for d in range(roots, late_from):
            copy_to(jnp.int32(d)).start()

        pl.semaphore_wait(complete, 1)
        for d in others(late_from, n):
            copy_to(d).start()

    for fetch in fetches[2:]:
        fetch.wait()
    width = counts_ref.shape[1]
    first_own = me * own

    def near(ref):
        found = ref[:, :LANES]
        for b in range(1, width // LANES):
            found = jnp.where(first_own // LANES == b, ref[:, LANES * b : LANES * (b + 1)], found)
        return found

    lists, counts, offsets = near(lists_ref), near(counts_ref), near(offsets_ref)
    station = lax.broadcasted_iota(jnp.int32, (n, LANES), 0)
    lane = lax.broadcasted_iota(jnp.int32, (n, LANES), 1)
    table = jnp.zeros((n, LANES), jnp.int32)
    for k in range(lists_ref.shape[0]):
        match = (lists[k : k + 1, :] == station) & (k < counts)
        table = table + jnp.where(match, offsets[k : k + 1, :] + 256, 0)
    here = lax.rem(first_own, LANES)
    for g in range(groups):
        for v in range(SUB):
            group = lax.bitwise_xor(lane // LAGS, v)
            code = jnp.take_along_axis(table, here + SUB * g + group, axis=1, mode="promise_in_bounds")
            sources[g, v] = LAGS * group + ((lane + code) & (LAGS - 1))
            if v == 0:
                lane_codes[g] = code

    def arrival(semaphore, count):
        some = slots.at[pl.ds(0, count)]
        return pltpu.make_async_copy(some, some, semaphore)

    def stage(sender):
        samples = slots[sender].astype(F32)
        for b in range(blocks):
            first_row = pl.multiple_of(sender * station_rows + ROWS * b, ROWS)
            staged[pl.ds(first_row, NCH), :] = samples[:, LANES * b : LANES * (b + 1)]

    lane = lax.broadcasted_iota(jnp.int32, (ROWS, LANES), 1)
    sub = lax.broadcasted_iota(jnp.int32, (ROWS, LANES), 0)
    inner = lane & (LAGS - 1)
    lane_group = lane // LAGS
    octets = n // ROWS
    out_parts = NTAU // LAGS
    out_blocks = NTAU // LANES

    totals[...] = jnp.zeros_like(totals)

    @pl.loop(0, octets)
    def work_off(turn):
        first = jnp.where(early, turn, octets - 1 - turn) * ROWS

        octet = first // ROWS
        here_rows = pl.ds(pl.multiple_of(first, ROWS), ROWS)
        masked = [
            [
                jnp.where(lane_codes[g, here_rows, :] >= 256, factors_ref[c, :, LANES * g : LANES * (g + 1)], 0.0)
                for g in range(groups)
            ]
            for c in range(NCH)
        ]
        pl.when(me // ROWS == octet)(arrival(recv_sem.at[octet], ROWS - 1).wait)
        pl.when(me // ROWS != octet)(arrival(recv_sem.at[octet], ROWS).wait)
        for i in range(ROWS):
            stage(first + i)

        parts = [
            [staged[pl.ds(first * station_rows + ROWS * b + c, ROWS, stride=station_rows), :] for b in range(blocks)]
            for c in range(NCH)
        ]

        squares = [[x * x for x in parts[c]] for c in range(NCH)]
        inside = [
            [
                [
                    jnp.sum(functools.reduce(jnp.add, x[b + 1 : b + wave_blocks]), axis=1, keepdims=True)
                    for x in (parts[c], squares[c])
                ]
                for b in range(lag_blocks)
            ]
            for c in range(NCH)
        ]
        pieces = []
        for b in range(blocks):
            rows = [parts[c][b] for c in range(NCH)]
            for c in range(NCH):
                square = squares[c][b]
                high = square.astype(BF16).astype(F32)
                rows += [high, square - high]
            rows.append(rows[0])
            pieces.append(jnp.concatenate(rows, axis=0).astype(BF16))
        stacked = jnp.concatenate(
            [jnp.concatenate([pieces[b], pieces[b + wave_blocks]], axis=1) for b in range(lag_blocks)], axis=0
        )
        sums = jnp.dot(stacked, window_ref[...], preferred_element_type=F32)
        held = ROWS * (3 * NCH + 1)

        inverses = [[] for _ in range(NCH)]
        for c in range(NCH):
            for b in range(lag_blocks):
                base = held * b
                whole, whole_squares = inside[c][b]
                mean_one = (sums[base + ROWS * c : base + ROWS * (c + 1)] + whole) / L
                at = base + ROWS * (NCH + 2 * c)
                mean_two = (sums[at : at + ROWS] + sums[at + ROWS : at + 2 * ROWS] + whole_squares) / L
                inverses[c].append(lax.rsqrt(mean_two - mean_one * mean_one + 1e-05))

        fitted = [[None] * groups for _ in range(parts_of_lags)]
        for c in range(NCH):
            shifted = [parts[c]]
            for j in range(1, SUB):
                rolled = [pltpu.roll(x, LANES - LAGS * j, 1) for x in parts[c]]
                stays = lane < LANES - LAGS * j
                shifted.append(
                    [jnp.where(stays, rolled[b], rolled[b + 1]) for b in range(blocks - 1)] + [rolled[-1]]
                )
            packed = [
                [jnp.concatenate([shifted[j][b], shifted[j + 1][b]], axis=0).astype(BF16) for b in range(blocks)]
                for j in range(0, SUB, 2)
            ]
            operand = jnp.concatenate(
                [
                    jnp.concatenate(packed[j][b : b + wave_blocks + 1], axis=1)
                    for b in range(lag_blocks)
                    for j in range(SUB // 2)
                ],
                axis=0,
            )
            products = jnp.dot(operand, bands[c], preferred_element_type=F32)
            for b in range(lag_blocks):
                inverse = inverses[c][b]
                for j in range(SUB):
                    k = SUB * b + j
                    spread = jnp.take_along_axis(inverse, inner + LAGS * j, axis=1, mode="promise_in_bounds")
                    for g in range(groups):
                        lanes = slice(LANES * g, LANES * (g + 1))
                        term = products[ROWS * k : ROWS * (k + 1), lanes] * (spread * masked[c][g])
                        fitted[k][g] = term if c == 0 else fitted[k][g] + term

        for g in range(groups):
            code = lane_codes[g, here_rows, :]
            far, half = (code & 64) != 0, (code & 32) != 0
            wraps = inner < (code & (LAGS - 1))
            one = [jnp.where(far, fitted[k + 2][g], fitted[k][g]) for k in range(out_parts + 2)]
            two = [jnp.where(half, one[k + 1], one[k]) for k in range(out_parts + 1)]
            picked = [jnp.where(wraps, two[k + 1], two[k]) for k in range(out_parts)]
            for b in range(out_blocks):
                mixed = picked[SUB * b : SUB * (b + 1)]
                for bit in (1, 2):
                    flipped = (lane_group & bit) != 0
                    mixed = [jnp.where(flipped, mixed[v ^ bit], mixed[v]) for v in range(SUB)]
                for v in range(SUB):
                    moved = jnp.take_along_axis(mixed[v], sources[g, v, here_rows, :], axis=1, mode="promise_in_bounds")
                    totals[b, g, v] += moved

    arrival(send_sem, n - 1).wait()

    for b in range(out_blocks):
        level = [totals[b, g, v] for g in range(groups) for v in range(SUB)]
        distance = 1
        while distance < ROWS:
            low = (sub & distance) == 0
            if distance < SUB:
                low = low == ((lane_group & distance) == 0)
            level = [
                jnp.where(low, x, y) + pltpu.roll(jnp.where(low, y, x), distance, 0)
                for x, y in zip(level[::2], level[1::2])
            ]
            distance *= 2
        out_ref[:, LANES * b : LANES * (b + 1)] = level[0]


def body(n, data, templates, station_lists, counts, offsets):
    own, _, length = templates.shape
    operands = (data, jnp.transpose(templates, (1, 0, 2)), station_lists, counts[None, :], offsets)
    return pl.pallas_call(
        functools.partial(network_kernel, n),
        out_shape=jax.ShapeDtypeStruct((own, NTAU), F32),
        in_specs=[pl.BlockSpec(memory_space=pltpu.HBM)] * len(operands),
        out_specs=pl.BlockSpec(memory_space=pltpu.VMEM),
        scratch_shapes=[pltpu.VMEM(x.shape, x.dtype) for x in operands[1:]]
        + [
            pltpu.VMEM((n, *data.shape[1:]), data.dtype),
            pltpu.VMEM(((n + 1) * ROWS * (data.shape[2] // LANES), LANES), F32),
            pltpu.VMEM((NCH, length + LANES, own * LAGS), BF16),
            pltpu.VMEM((NCH, ROWS, own * LAGS), F32),
            pltpu.VMEM((2 * LANES, LANES), BF16),
            pltpu.VMEM((own // SUB, n, LANES), jnp.int32),
            pltpu.VMEM((own // SUB, SUB, n, LANES), jnp.int32),
            pltpu.VMEM((NTAU // LANES, own // SUB, SUB, ROWS, LANES), F32),
            pltpu.SemaphoreType.DMA((len(operands),)),
            pltpu.SemaphoreType.DMA,
            pltpu.SemaphoreType.DMA((n // ROWS,)),
            pltpu.SemaphoreType.REGULAR((2,)),
            pltpu.SemaphoreType.REGULAR,
        ],
        compiler_params=pltpu.CompilerParams(
            collective_id=0, has_side_effects=True, vmem_limit_bytes=40 * 1024 * 1024
        ),
    )(*[pltpu.with_memory_space_constraint(x, pltpu.HBM) for x in operands])


def solution(mesh):
    placed = (P(("parts", "sta"), None, None), P("sta", None, None), P(), P(), P())
    return jax.shard_map(
        functools.partial(body, mesh.shape["sta"]), mesh=mesh, in_specs=placed,
        out_specs=P(("parts", "sta"), None), check_vma=False,
    )
```

```python
import functools

import jax
import jax.numpy as jnp
from jax import lax
from jax.experimental import pallas as pl
from jax.experimental.pallas import tpu as pltpu
from jax.sharding import PartitionSpec as P

NCH = 3
L = 512
NTAU = 256
LANES = 128
ROWS = 8
LAGS = 32
SUB = LANES // LAGS
F32 = jnp.float32
BF16 = jnp.bfloat16
MESH = pl.DeviceIdType.MESH


def network_kernel(
    n, data_hbm, templates_hbm, lists_hbm, counts_hbm, offsets_hbm, out_ref,
    templates_ref, lists_ref, counts_ref, offsets_ref,
    slots, staged, bands, factors_ref, window_ref, lane_codes, sources, totals,
    fetch_sem, send_sem, recv_sem, joined, complete,
):
    me = lax.axis_index("sta")
    fetches = [
        pltpu.make_async_copy(source, target, fetch_sem.at[i])
        for i, (source, target) in enumerate(
            [
                (data_hbm.at[0], slots.at[me]), (templates_hbm, templates_ref), (lists_hbm, lists_ref),
                (counts_hbm, counts_ref), (offsets_hbm, offsets_ref),
            ]
        )
    ]
    samples_len = data_hbm.shape[2]
    blocks = samples_len // LANES
    lag_blocks = (samples_len - L) // LANES
    wave_blocks = L // LANES
    own = templates_ref.shape[1]
    groups = own // SUB
    station_rows = ROWS * blocks
    parts_of_lags = lag_blocks * SUB

    gap = n // 4
    late_from = n - gap
    roots = 2
    early = me < late_from
    barrier = pltpu.get_barrier_semaphore()

    def others(low, high):
        return [d + jnp.where(me <= d, 1, 0).astype(jnp.int32) for d in range(low, high - 1)]

    def tell(semaphore, d):
        pl.semaphore_signal(semaphore, inc=1, device_id={"sta": d}, device_id_type=MESH)

    direct = late_from + gap // 2
    far_from = late_from - gap

    @pl.when(me < roots)
    def _():
        for d in reversed(range(direct, n)):
            tell(barrier, jnp.int32(d))

    def copy_to(target, source=slots.at[me]):
        return pltpu.make_async_remote_copy(
            src_ref=source,
            dst_ref=slots.at[me],
            send_sem=send_sem,
            recv_sem=recv_sem.at[me // ROWS],
            device_id={"sta": target},
            device_id_type=MESH,
        )

    @pl.when(me >= direct)
    def _():
        pl.semaphore_wait(barrier, roots)
        for d in range(roots):
            copy_to(jnp.int32(d), data_hbm.at[0]).start()
            tell(joined.at[1], jnp.int32(d))

    fetches[0].start()

    @pl.when(early)
    def _():
        for d in range(late_from, direct):
            tell(barrier, jnp.int32(d))
        for d in others(0, late_from):
            tell(barrier, d)

    for fetch in fetches[1:]:
        fetch.start()

    @pl.when(early)
    def _():
        fetches[0].wait()
        pl.semaphore_wait(barrier, late_from - 1)

        @pl.when((me + gap >= direct) & (me + gap < n))
        def _():
            tell(barrier, me + gap)

        @pl.when(me < far_from)
        def _():
            for d in others(0, late_from):
                copy_to(d).start()

        @pl.when(me >= far_from)
        def _():
            for d in range(roots):
                copy_to(jnp.int32(d)).start()
            for d in others(far_from, late_from):
                copy_to(d).start()

    @pl.when(jnp.logical_not(early))
    def _():
        @pl.when(me < direct)
        def _():
            fetches[0].wait()
            pl.semaphore_wait(barrier, late_from)
            for d in range(late_from):
                tell(joined.at[0], jnp.int32(d))
                if d < roots:
                    copy_to(jnp.int32(d)).start()

        @pl.when(me >= direct)
        def _():
            fetches[0].wait()
            pl.semaphore_wait(barrier, 1)
            for d in range(roots, late_from):
                tell(joined.at[1], jnp.int32(d))
                copy_to(jnp.int32(d)).start()

    window_row = lax.broadcasted_iota(jnp.int32, (2 * LANES, LANES), 0)
    window_lane = lax.broadcasted_iota(jnp.int32, (2 * LANES, LANES), 1)
    window = ((window_row >= window_lane) & (window_row < window_lane + LANES)).astype(F32)
    window_ref[...] = window.astype(BF16)

    fetches[1].wait()
    band_row = lax.broadcasted_iota(jnp.int32, (LAGS, LANES), 0)
    band_lane = lax.broadcasted_iota(jnp.int32, (LAGS, LANES), 1)
    upper = band_lane >= band_row
    owner_row = lax.broadcasted_iota(jnp.int32, (own, own * LAGS), 0)
    owner_lane = lax.broadcasted_iota(jnp.int32, (own, own * LAGS), 1) // LAGS
    for c in range(NCH):
        values = templates_ref[c].astype(F32)
        mean = jnp.sum(values, axis=1, keepdims=True) / L
        centered = (values - mean).astype(BF16).astype(F32)
        power = jnp.sum(centered * centered, axis=1, keepdims=True) / L
        factor = 1.0 / (NCH * L * jnp.sqrt(power + 1e-06))
        row = jnp.sum(jnp.where(owner_row == owner_lane, factor, 0.0), axis=0, keepdims=True)
        factors_ref[c] = jnp.broadcast_to(row, (ROWS, own * LAGS))
        before = [jnp.zeros((LAGS, LANES), F32)] * own
        for k in range(wave_blocks + 1):
            if k < wave_blocks:
                turned = [
                    pltpu.roll(
                        jnp.broadcast_to(centered[t : t + 1, LANES * k : LANES * (k + 1)], (LAGS, LANES)),
                        0, 1, stride=1, stride_axis=0,
                    )
                    for t in range(own)
                ]
            else:
                turned = [jnp.zeros((LAGS, LANES), F32)] * own
            for g in range(groups):
                merged = jnp.concatenate(
                    [jnp.where(upper, turned[t], before[t]) for t in range(SUB * g, SUB * (g + 1))], axis=0
                )
                bands[c, LANES * k : LANES * (k + 1), LANES * g : LANES * (g + 1)] = merged.T.astype(BF16)
            before = turned

    @pl.when(early)
    def _():
        @pl.when(me >= far_from)
        def _():
            for d in range(roots, far_from):
                copy_to(jnp.int32(d)).start()

        pl.semaphore_wait(joined.at[0], direct - late_from)
        for d in reversed(range(late_from, direct)):
            copy_to(jnp.int32(d)).start()

    @pl.when(early)
    def _():
        pl.semaphore_wait(joined.at[1], n - direct)

        @pl.when(me >= far_from)
        def _():
            tell(complete, me + gap)

        for d in range(direct, n):
            copy_to(jnp.int32(d)).start()

    @pl.when(jnp.logical_not(early))
    def _():
        @pl.when(me < direct)
        def _():
            for d in range(roots, late_from):
                copy_to(jnp.int32(d)).start()

        pl.semaphore_wait(complete, 1)
        for d in others(late_from, n):
            copy_to(d).start()

    for fetch in fetches[2:]:
        fetch.wait()
    width = counts_ref.shape[1]
    first_own = me * own

    def near(ref):
        found = ref[:, :LANES]
        for b in range(1, width // LANES):
            found = jnp.where(first_own // LANES == b, ref[:, LANES * b : LANES * (b + 1)], found)
        return found

    lists, counts, offsets = near(lists_ref), near(counts_ref), near(offsets_ref)
    station = lax.broadcasted_iota(jnp.int32, (n, LANES), 0)
    lane = lax.broadcasted_iota(jnp.int32, (n, LANES), 1)
    table = jnp.zeros((n, LANES), jnp.int32)
    for k in range(lists_ref.shape[0]):
        match = (lists[k : k + 1, :] == station) & (k < counts)
        table = table + jnp.where(match, offsets[k : k + 1, :] + 256, 0)
    here = lax.rem(first_own, LANES)
    for g in range(groups):
        for v in range(SUB):
            group = lax.bitwise_xor(lane // LAGS, v)
            code = jnp.take_along_axis(table, here + SUB * g + group, axis=1, mode="promise_in_bounds")
            sources[g, v] = LAGS * group + ((lane + code) & (LAGS - 1))
            if v == 0:
                lane_codes[g] = code

    def arrival(semaphore, count):
        some = slots.at[pl.ds(0, count)]
        return pltpu.make_async_copy(some, some, semaphore)

    def stage(sender):
        samples = slots[sender].astype(F32)
        for b in range(blocks):
            first_row = pl.multiple_of(sender * station_rows + ROWS * b, ROWS)
            staged[pl.ds(first_row, NCH), :] = samples[:, LANES * b : LANES * (b + 1)]

    lane = lax.broadcasted_iota(jnp.int32, (ROWS, LANES), 1)
    sub = lax.broadcasted_iota(jnp.int32, (ROWS, LANES), 0)
    inner = lane & (LAGS - 1)
    lane_group = lane // LAGS
    octets = n // ROWS
    out_parts = NTAU // LAGS
    out_blocks = NTAU // LANES

    totals[...] = jnp.zeros_like(totals)

    for turn in range(octets):
        first = jnp.where(early, turn, octets - 1 - turn) * ROWS

        octet = first // ROWS
        here_rows = pl.ds(pl.multiple_of(first, ROWS), ROWS)
        masked = [
            [
                jnp.where(lane_codes[g, here_rows, :] >= 256, factors_ref[c, :, LANES * g : LANES * (g + 1)], 0.0)
                for g in range(groups)
            ]
            for c in range(NCH)
        ]
        pl.when(me // ROWS == octet)(arrival(recv_sem.at[octet], ROWS - 1).wait)
        pl.when(me // ROWS != octet)(arrival(recv_sem.at[octet], ROWS).wait)
        for i in range(ROWS):
            stage(first + i)

        parts = [
            [staged[pl.ds(first * station_rows + ROWS * b + c, ROWS, stride=station_rows), :] for b in range(blocks)]
            for c in range(NCH)
        ]

        squares = [[x * x for x in parts[c]] for c in range(NCH)]
        inside = [
            [
                [
                    jnp.sum(functools.reduce(jnp.add, x[b + 1 : b + wave_blocks]), axis=1, keepdims=True)
                    for x in (parts[c], squares[c])
                ]
                for b in range(lag_blocks)
            ]
            for c in range(NCH)
        ]
        pieces = []
        for b in range(blocks):
            rows = [parts[c][b] for c in range(NCH)]
            for c in range(NCH):
                square = squares[c][b]
                high = square.astype(BF16).astype(F32)
                rows += [high, square - high]
            rows.append(rows[0])
            pieces.append(jnp.concatenate(rows, axis=0).astype(BF16))
        stacked = jnp.concatenate(
            [jnp.concatenate([pieces[b], pieces[b + wave_blocks]], axis=1) for b in range(lag_blocks)], axis=0
        )
        sums = jnp.dot(stacked, window_ref[...], preferred_element_type=F32)
        held = ROWS * (3 * NCH + 1)

        inverses = [[] for _ in range(NCH)]
        for c in range(NCH):
            for b in range(lag_blocks):
                base = held * b
                whole, whole_squares = inside[c][b]
                mean_one = (sums[base + ROWS * c : base + ROWS * (c + 1)] + whole) / L
                at = base + ROWS * (NCH + 2 * c)
                mean_two = (sums[at : at + ROWS] + sums[at + ROWS : at + 2 * ROWS] + whole_squares) / L
                inverses[c].append(lax.rsqrt(mean_two - mean_one * mean_one + 1e-05))

        fitted = [[None] * groups for _ in range(parts_of_lags)]
        for c in range(NCH):
            shifted = [parts[c]]
            for j in range(1, SUB):
                rolled = [pltpu.roll(x, LANES - LAGS * j, 1) for x in parts[c]]
                stays = lane < LANES - LAGS * j
                shifted.append(
                    [jnp.where(stays, rolled[b], rolled[b + 1]) for b in range(blocks - 1)] + [rolled[-1]]
                )
            packed = [
                [jnp.concatenate([shifted[j][b], shifted[j + 1][b]], axis=0).astype(BF16) for b in range(blocks)]
                for j in range(0, SUB, 2)
            ]
            operand = jnp.concatenate(
                [
                    jnp.concatenate(packed[j][b : b + wave_blocks + 1], axis=1)
                    for b in range(lag_blocks)
                    for j in range(SUB // 2)
                ],
                axis=0,
            )
            products = jnp.dot(operand, bands[c], preferred_element_type=F32)
            for b in range(lag_blocks):
                inverse = inverses[c][b]
                for j in range(SUB):
                    k = SUB * b + j
                    spread = jnp.take_along_axis(inverse, inner + LAGS * j, axis=1, mode="promise_in_bounds")
                    for g in range(groups):
                        lanes = slice(LANES * g, LANES * (g + 1))
                        term = products[ROWS * k : ROWS * (k + 1), lanes] * (spread * masked[c][g])
                        fitted[k][g] = term if c == 0 else fitted[k][g] + term

        for g in range(groups):
            code = lane_codes[g, here_rows, :]
            far, half = (code & 64) != 0, (code & 32) != 0
            wraps = inner < (code & (LAGS - 1))
            one = [jnp.where(far, fitted[k + 2][g], fitted[k][g]) for k in range(out_parts + 2)]
            two = [jnp.where(half, one[k + 1], one[k]) for k in range(out_parts + 1)]
            picked = [jnp.where(wraps, two[k + 1], two[k]) for k in range(out_parts)]
            for b in range(out_blocks):
                mixed = picked[SUB * b : SUB * (b + 1)]
                for bit in (1, 2):
                    flipped = (lane_group & bit) != 0
                    mixed = [jnp.where(flipped, mixed[v ^ bit], mixed[v]) for v in range(SUB)]
                for v in range(SUB):
                    moved = jnp.take_along_axis(mixed[v], sources[g, v, here_rows, :], axis=1, mode="promise_in_bounds")
                    totals[b, g, v] += moved

    arrival(send_sem, n - 1).wait()

    for b in range(out_blocks):
        level = [totals[b, g, v] for g in range(groups) for v in range(SUB)]
        distance = 1
        while distance < ROWS:
            low = (sub & distance) == 0
            if distance < SUB:
                low = low == ((lane_group & distance) == 0)
            level = [
                jnp.where(low, x, y) + pltpu.roll(jnp.where(low, y, x), distance, 0)
                for x, y in zip(level[::2], level[1::2])
            ]
            distance *= 2
        out_ref[:, LANES * b : LANES * (b + 1)] = level[0]


def body(n, data, templates, station_lists, counts, offsets):
    own, _, length = templates.shape
    operands = (data, jnp.transpose(templates, (1, 0, 2)), station_lists, counts[None, :], offsets)
    return pl.pallas_call(
        functools.partial(network_kernel, n),
        out_shape=jax.ShapeDtypeStruct((own, NTAU), F32),
        in_specs=[pl.BlockSpec(memory_space=pltpu.HBM)] * len(operands),
        out_specs=pl.BlockSpec(memory_space=pltpu.VMEM),
        scratch_shapes=[pltpu.VMEM(x.shape, x.dtype) for x in operands[1:]]
        + [
            pltpu.VMEM((n, *data.shape[1:]), data.dtype),
            pltpu.VMEM(((n + 1) * ROWS * (data.shape[2] // LANES), LANES), F32),
            pltpu.VMEM((NCH, length + LANES, own * LAGS), BF16),
            pltpu.VMEM((NCH, ROWS, own * LAGS), F32),
            pltpu.VMEM((2 * LANES, LANES), BF16),
            pltpu.VMEM((own // SUB, n, LANES), jnp.int32),
            pltpu.VMEM((own // SUB, SUB, n, LANES), jnp.int32),
            pltpu.VMEM((NTAU // LANES, own // SUB, SUB, ROWS, LANES), F32),
            pltpu.SemaphoreType.DMA((len(operands),)),
            pltpu.SemaphoreType.DMA,
            pltpu.SemaphoreType.DMA((n // ROWS,)),
            pltpu.SemaphoreType.REGULAR((2,)),
            pltpu.SemaphoreType.REGULAR,
        ],
        compiler_params=pltpu.CompilerParams(
            collective_id=0, has_side_effects=True, vmem_limit_bytes=40 * 1024 * 1024
        ),
    )(*[pltpu.with_memory_space_constraint(x, pltpu.HBM) for x in operands])


def solution(mesh):
    placed = (P(("parts", "sta"), None, None), P("sta", None, None), P(), P(), P())
    return jax.shard_map(
        functools.partial(body, mesh.shape["sta"]), mesh=mesh, in_specs=placed,
        out_specs=P(("parts", "sta"), None), check_vma=False,
    )
```

```python
import functools

import jax
import jax.numpy as jnp
from jax import lax
from jax.experimental import pallas as pl
from jax.experimental.pallas import tpu as pltpu
from jax.sharding import PartitionSpec as P

NCH = 3
L = 512
NTAU = 256
LANES = 128
ROWS = 8
LAGS = 32
SUB = LANES // LAGS
F32 = jnp.float32
BF16 = jnp.bfloat16
MESH = pl.DeviceIdType.MESH


def network_kernel(
    n, data_hbm, templates_hbm, lists_hbm, counts_hbm, offsets_hbm, out_ref,
    templates_ref, lists_ref, counts_ref, offsets_ref,
    slots, staged, bands, factors_ref, window_ref, lane_codes, sources, totals,
    fetch_sem, send_sem, recv_sem, joined, complete,
):
    me = lax.axis_index("sta")
    fetches = [
        pltpu.make_async_copy(source, target, fetch_sem.at[i])
        for i, (source, target) in enumerate(
            [
                (data_hbm.at[0], slots.at[me]), (templates_hbm, templates_ref), (lists_hbm, lists_ref),
                (counts_hbm, counts_ref), (offsets_hbm, offsets_ref),
            ]
        )
    ]
    samples_len = data_hbm.shape[2]
    blocks = samples_len // LANES
    lag_blocks = (samples_len - L) // LANES
    wave_blocks = L // LANES
    own = templates_ref.shape[1]
    groups = own // SUB
    station_rows = ROWS * blocks
    parts_of_lags = lag_blocks * SUB

    gap = n // 4
    late_from = n - gap
    roots = 2
    early = me < late_from
    barrier = pltpu.get_barrier_semaphore()

    def others(low, high):
        return [d + jnp.where(me <= d, 1, 0).astype(jnp.int32) for d in range(low, high - 1)]

    def tell(semaphore, d):
        pl.semaphore_signal(semaphore, inc=1, device_id={"sta": d}, device_id_type=MESH)

    direct = late_from + gap // 2
    far_from = late_from - gap

    @pl.when(me < roots)
    def _():
        for d in reversed(range(direct, n)):
            tell(barrier, jnp.int32(d))

    def copy_to(target, source=slots.at[me]):
        return pltpu.make_async_remote_copy(
            src_ref=source,
            dst_ref=slots.at[me],
            send_sem=send_sem,
            recv_sem=recv_sem.at[me // ROWS],
            device_id={"sta": target},
            device_id_type=MESH,
        )

    @pl.when(me >= direct)
    def _():
        pl.semaphore_wait(barrier, roots)
        for d in range(roots):
            copy_to(jnp.int32(d), data_hbm.at[0]).start()
            tell(joined.at[1], jnp.int32(d))

    fetches[0].start()

    @pl.when(early)
    def _():
        for d in range(late_from, direct):
            tell(barrier, jnp.int32(d))
        for d in others(0, late_from):
            tell(barrier, d)

    for fetch in fetches[1:]:
        fetch.start()

    @pl.when(early)
    def _():
        fetches[0].wait()
        pl.semaphore_wait(barrier, late_from - 1)

        @pl.when((me + gap >= direct) & (me + gap < n))
        def _():
            tell(barrier, me + gap)

        @pl.when(me < far_from)
        def _():
            for d in others(0, late_from):
                copy_to(d).start()

        @pl.when(me >= far_from)
        def _():
            for d in range(roots):
                copy_to(jnp.int32(d)).start()
            for d in others(far_from, late_from):
                copy_to(d).start()

    @pl.when(jnp.logical_not(early))
    def _():
        @pl.when(me < direct)
        def _():
            fetches[0].wait()
            pl.semaphore_wait(barrier, late_from)
            for d in range(late_from):
                tell(joined.at[0], jnp.int32(d))
                if d < roots:
                    copy_to(jnp.int32(d)).start()

        @pl.when(me >= direct)
        def _():
            fetches[0].wait()
            pl.semaphore_wait(barrier, 1)
            for d in range(roots, late_from):
                tell(joined.at[1], jnp.int32(d))
                copy_to(jnp.int32(d)).start()

    window_row = lax.broadcasted_iota(jnp.int32, (2 * LANES, LANES), 0)
    window_lane = lax.broadcasted_iota(jnp.int32, (2 * LANES, LANES), 1)
    window = ((window_row >= window_lane) & (window_row < window_lane + LANES)).astype(F32)
    window_ref[...] = window.astype(BF16)

    fetches[1].wait()
    band_row = lax.broadcasted_iota(jnp.int32, (LAGS, LANES), 0)
    band_lane = lax.broadcasted_iota(jnp.int32, (LAGS, LANES), 1)
    upper = band_lane >= band_row
    owner_row = lax.broadcasted_iota(jnp.int32, (own, own * LAGS), 0)
    owner_lane = lax.broadcasted_iota(jnp.int32, (own, own * LAGS), 1) // LAGS
    for c in range(NCH):
        values = templates_ref[c].astype(F32)
        mean = jnp.sum(values, axis=1, keepdims=True) / L
        centered = (values - mean).astype(BF16).astype(F32)
        power = jnp.sum(centered * centered, axis=1, keepdims=True) / L
        factor = 1.0 / (NCH * L * jnp.sqrt(power + 1e-06))
        row = jnp.sum(jnp.where(owner_row == owner_lane, factor, 0.0), axis=0, keepdims=True)
        factors_ref[c] = jnp.broadcast_to(row, (ROWS, own * LAGS))
        before = [jnp.zeros((LAGS, LANES), F32)] * own
        for k in range(wave_blocks + 1):
            if k < wave_blocks:
                turned = [
                    pltpu.roll(
                        jnp.broadcast_to(centered[t : t + 1, LANES * k : LANES * (k + 1)], (LAGS, LANES)),
                        0, 1, stride=1, stride_axis=0,
                    )
                    for t in range(own)
                ]
            else:
                turned = [jnp.zeros((LAGS, LANES), F32)] * own
            for g in range(groups):
                merged = jnp.concatenate(
                    [jnp.where(upper, turned[t], before[t]) for t in range(SUB * g, SUB * (g + 1))], axis=0
                )
                bands[c, LANES * k : LANES * (k + 1), LANES * g : LANES * (g + 1)] = merged.T.astype(BF16)
            before = turned

    @pl.when(early)
    def _():
        @pl.when(me >= far_from)
        def _():
            for d in range(roots, far_from):
                copy_to(jnp.int32(d)).start()

        pl.semaphore_wait(joined.at[0], direct - late_from)
        for d in reversed(range(late_from, direct)):
            copy_to(jnp.int32(d)).start()

    @pl.when(early)
    def _():
        pl.semaphore_wait(joined.at[1], n - direct)

        @pl.when(me >= far_from)
        def _():
            tell(complete, me + gap)

        for d in range(direct, n):
            copy_to(jnp.int32(d)).start()

    @pl.when(jnp.logical_not(early))
    def _():
        @pl.when(me < direct)
        def _():
            for d in range(roots, late_from):
                copy_to(jnp.int32(d)).start()

        pl.semaphore_wait(complete, 1)
        for d in others(late_from, n):
            copy_to(d).start()

    for fetch in fetches[2:]:
        fetch.wait()
    width = counts_ref.shape[1]
    first_own = me * own

    def near(ref):
        found = ref[:, :LANES]
        for b in range(1, width // LANES):
            found = jnp.where(first_own // LANES == b, ref[:, LANES * b : LANES * (b + 1)], found)
        return found

    lists, counts, offsets = near(lists_ref), near(counts_ref), near(offsets_ref)
    station = lax.broadcasted_iota(jnp.int32, (n, LANES), 0)
    lane = lax.broadcasted_iota(jnp.int32, (n, LANES), 1)
    table = jnp.zeros((n, LANES), jnp.int32)
    for k in range(lists_ref.shape[0]):
        match = (lists[k : k + 1, :] == station) & (k < counts)
        table = table + jnp.where(match, offsets[k : k + 1, :] + 256, 0)
    here = lax.rem(first_own, LANES)
    for g in range(groups):
        for v in range(SUB):
            group = lax.bitwise_xor(lane // LAGS, v)
            code = jnp.take_along_axis(table, here + SUB * g + group, axis=1, mode="promise_in_bounds")
            sources[g, v] = LAGS * group + ((lane + code) & (LAGS - 1))
            if v == 0:
                lane_codes[g] = code

    def arrival(semaphore, count):
        some = slots.at[pl.ds(0, count)]
        return pltpu.make_async_copy(some, some, semaphore)

    def stage(sender):
        samples = slots[sender].astype(F32)
        for b in range(blocks):
            first_row = pl.multiple_of(sender * station_rows + ROWS * b, ROWS)
            staged[pl.ds(first_row, NCH), :] = samples[:, LANES * b : LANES * (b + 1)]

    lane = lax.broadcasted_iota(jnp.int32, (ROWS, LANES), 1)
    sub = lax.broadcasted_iota(jnp.int32, (ROWS, LANES), 0)
    inner = lane & (LAGS - 1)
    lane_group = lane // LAGS
    octets = n // ROWS
    out_parts = NTAU // LAGS
    out_blocks = NTAU // LANES

    totals[...] = jnp.zeros_like(totals)

    @pl.loop(0, octets)
    def work_off(turn):
        first = jnp.where(early, turn, octets - 1 - turn) * ROWS

        octet = first // ROWS
        here_rows = pl.ds(pl.multiple_of(first, ROWS), ROWS)
        masked = [
            [
                jnp.where(lane_codes[g, here_rows, :] >= 256, factors_ref[c, :, LANES * g : LANES * (g + 1)], 0.0)
                for g in range(groups)
            ]
            for c in range(NCH)
        ]
        pl.when(me // ROWS == octet)(arrival(recv_sem.at[octet], ROWS - 1).wait)
        pl.when(me // ROWS != octet)(arrival(recv_sem.at[octet], ROWS).wait)
        for i in range(ROWS):
            stage(first + i)

        parts = [
            [staged[pl.ds(first * station_rows + ROWS * b + c, ROWS, stride=station_rows), :] for b in range(blocks)]
            for c in range(NCH)
        ]

        squares = [[x * x for x in parts[c]] for c in range(NCH)]
        inside = [
            [
                [
                    jnp.sum(functools.reduce(jnp.add, x[b + 1 : b + wave_blocks]), axis=1, keepdims=True)
                    for x in (parts[c], squares[c])
                ]
                for b in range(lag_blocks)
            ]
            for c in range(NCH)
        ]
        pieces = []
        for b in range(blocks):
            rows = [parts[c][b] for c in range(NCH)]
            for c in range(NCH):
                square = squares[c][b]
                high = square.astype(BF16).astype(F32)
                rows += [high, square - high]
            rows.append(rows[0])
            pieces.append(jnp.concatenate(rows, axis=0).astype(BF16))
        stacked = jnp.concatenate(
            [jnp.concatenate([pieces[b], pieces[b + wave_blocks]], axis=1) for b in range(lag_blocks)], axis=0
        )
        sums = jnp.dot(stacked, window_ref[...], preferred_element_type=F32)
        held = ROWS * (3 * NCH + 1)

        inverses = [[] for _ in range(NCH)]
        for c in range(NCH):
            for b in range(lag_blocks):
                base = held * b
                whole, whole_squares = inside[c][b]
                mean_one = (sums[base + ROWS * c : base + ROWS * (c + 1)] + whole) / L
                at = base + ROWS * (NCH + 2 * c)
                mean_two = (sums[at : at + ROWS] + sums[at + ROWS : at + 2 * ROWS] + whole_squares) / L
                inverses[c].append(lax.rsqrt(mean_two - mean_one * mean_one + 1e-05))

        fitted = [[None] * groups for _ in range(parts_of_lags)]
        for c in range(NCH):
            shifted = [parts[c]]
            for j in range(1, SUB):
                rolled = [pltpu.roll(x, LANES - LAGS * j, 1) for x in parts[c]]
                stays = lane < LANES - LAGS * j
                shifted.append(
                    [jnp.where(stays, rolled[b], rolled[b + 1]) for b in range(blocks - 1)] + [rolled[-1]]
                )
            packed = [
                [jnp.concatenate([shifted[j][b], shifted[j + 1][b]], axis=0).astype(BF16) for b in range(blocks)]
                for j in range(0, SUB, 2)
            ]
            operand = jnp.concatenate(
                [
                    jnp.concatenate(packed[j][b : b + wave_blocks + 1], axis=1)
                    for b in range(lag_blocks)
                    for j in range(SUB // 2)
                ],
                axis=0,
            )
            products = jnp.dot(operand, bands[c], preferred_element_type=F32)
            for b in range(lag_blocks):
                inverse = inverses[c][b]
                for j in range(SUB):
                    k = SUB * b + j
                    spread = jnp.take_along_axis(inverse, inner + LAGS * j, axis=1, mode="promise_in_bounds")
                    for g in range(groups):
                        lanes = slice(LANES * g, LANES * (g + 1))
                        term = products[ROWS * k : ROWS * (k + 1), lanes] * (spread * masked[c][g])
                        fitted[k][g] = term if c == 0 else fitted[k][g] + term

        for g in range(groups):
            code = lane_codes[g, here_rows, :]
            far, half = (code & 64) != 0, (code & 32) != 0
            wraps = inner < (code & (LAGS - 1))
            one = [jnp.where(far, fitted[k + 2][g], fitted[k][g]) for k in range(out_parts + 2)]
            two = [jnp.where(half, one[k + 1], one[k]) for k in range(out_parts + 1)]
            picked = [jnp.where(wraps, two[k + 1], two[k]) for k in range(out_parts)]
            for b in range(out_blocks):
                mixed = picked[SUB * b : SUB * (b + 1)]
                for bit in (1, 2):
                    flipped = (lane_group & bit) != 0
                    mixed = [jnp.where(flipped, mixed[v ^ bit], mixed[v]) for v in range(SUB)]
                for v in range(SUB):
                    moved = jnp.take_along_axis(mixed[v], sources[g, v, here_rows, :], axis=1, mode="promise_in_bounds")
                    totals[b, g, v] += moved

    arrival(send_sem, n - 1).wait()

    for b in range(out_blocks):
        level = [totals[b, g, v] for g in range(groups) for v in range(SUB)]
        distance = 1
        while distance < ROWS:
            low = (sub & distance) == 0
            if distance < SUB:
                low = low == ((lane_group & distance) == 0)
            level = [
                jnp.where(low, x, y) + pltpu.roll(jnp.where(low, y, x), distance, 0)
                for x, y in zip(level[::2], level[1::2])
            ]
            distance *= 2
        out_ref[:, LANES * b : LANES * (b + 1)] = level[0]


def body(n, data, templates, station_lists, counts, offsets):
    own, _, length = templates.shape
    operands = (data, jnp.transpose(templates, (1, 0, 2)), station_lists, counts[None, :], offsets)
    return pl.pallas_call(
        functools.partial(network_kernel, n),
        out_shape=jax.ShapeDtypeStruct((own, NTAU), F32),
        in_specs=[pl.BlockSpec(memory_space=pltpu.HBM)] * len(operands),
        out_specs=pl.BlockSpec(memory_space=pltpu.VMEM),
        scratch_shapes=[pltpu.VMEM(x.shape, x.dtype) for x in operands[1:]]
        + [
            pltpu.VMEM((n, *data.shape[1:]), data.dtype),
            pltpu.VMEM(((n + 1) * ROWS * (data.shape[2] // LANES), LANES), F32),
            pltpu.VMEM((NCH, length + LANES, own * LAGS), BF16),
            pltpu.VMEM((NCH, ROWS, own * LAGS), F32),
            pltpu.VMEM((2 * LANES, LANES), BF16),
            pltpu.VMEM((own // SUB, n, LANES), jnp.int32),
            pltpu.VMEM((own // SUB, SUB, n, LANES), jnp.int32),
            pltpu.VMEM((NTAU // LANES, own // SUB, SUB, ROWS, LANES), F32),
            pltpu.SemaphoreType.DMA((len(operands),)),
            pltpu.SemaphoreType.DMA,
            pltpu.SemaphoreType.DMA((n // ROWS,)),
            pltpu.SemaphoreType.REGULAR((2,)),
            pltpu.SemaphoreType.REGULAR,
        ],
        compiler_params=pltpu.CompilerParams(
            collective_id=0, has_side_effects=True, vmem_limit_bytes=40 * 1024 * 1024
        ),
    )(*[pltpu.with_memory_space_constraint(x, pltpu.HBM) for x in operands])


def solution(mesh):
    placed = (P(("parts", "sta"), None, None), P("sta", None, None), P(), P(), P())
    return jax.shard_map(
        functools.partial(body, mesh.shape["sta"]), mesh=mesh, in_specs=placed,
        out_specs=P(("parts", "sta"), None), check_vma=False,
    )
```
